256 devices in a mesh: tm: 32 (over y, z), azi: 2 (over x_hi), rad: 4 (over x_lo, core).
Axes of the slice: x: 4 (x_hi: 2, x_lo: 2; x = x_hi * 2 + x_lo), y: 4, z: 8, core: 2. Of those that a mesh axis runs over, the one named last changes fastest.
Arguments:
- start_states: float32 [32, 64, 32, 128], P('tm', 'rad', 'azi'), may hold values from -6 to 6
- target: float32 [32, 64, 32, 128], P('tm', 'rad', 'azi'), may hold values from -6 to 6
- conductivity: float32 [64, 32, 128], P('rad', 'azi'), may hold values from 0.1 to 1000
- material: int32 [64, 32, 128], P('rad', 'azi'), may hold values from 0 to 2
- current: float32 [64, 32, 128], P('rad', 'azi'), may hold values from -6 to 6
- bh_coef: float32 [3], replicated, may hold values from 0.05 to 0.5
Outputs:
- new_end: float32 [32, 64, 32, 128], P('tm', 'rad', 'azi')
- grad_conductivity: float32 [64, 32, 128], P('rad', 'azi')
- bh_grad: float32 [3], replicated
The draws below stay inside these ranges and needn't reach their ends.
Inputs may be any that keep to these rules, and one draw needn't show every extreme that they name: `material`: 0 marks air, 1 iron, 2 copper.
All inputs are finite; a program needn't handle non-finite values.
Results may differ from the reference program's by a relative error of at most 0.00011.
Values sent between devices are 32-bit elements; how exact they have to be, the bound alone decides.
No kernel may reach another device: no remote copies, remote signals or barrier semaphores. Data moves between devices by JAX's collectives and lax.ppermute only.
A program may use at most 64 MiB of HBM per device.

```python
import math
import jax
import jax.numpy as jnp
from jax import lax

NZ = 128
STEPS = 2
SWEEPS = 8
NR = 64
NA = 32
SLICES = 32


def set_ends(drawn, stream_key, smallest, high):
    spot = [jax.random.randint(jax.random.fold_in(stream_key, axis), (), 0, length) for axis, length in enumerate(drawn.shape)]
    main_axis = drawn.shape.index(max(drawn.shape))
    next_to = spot[:main_axis] + [(spot[main_axis] + 1) % drawn.shape[main_axis]] + spot[main_axis + 1:]
    return drawn.at[tuple(spot)].set(smallest).at[tuple(next_to)].set(high)


def block_scale(stream_key, dims, split, smallest, largest):
    factor_of, own = 1.0, jax.random.fold_in(stream_key, 6)
    for position, blocks in split:
        draws = jnp.exp(jax.random.uniform(jax.random.fold_in(own, position), (blocks,), jnp.float32, smallest / len(split), largest / len(split)))
        factor_of = factor_of * jnp.repeat(draws, dims[position] // blocks).reshape([-1 if axis == position else 1 for axis in range(len(dims))])
    return factor_of


def gaussian(rng, shape, scale, bound, shards=(), kind=jnp.bfloat16):
    values = jax.random.normal(rng, shape, jnp.float32) * scale
    if len(shards) > 0:
        values = block_scale(rng, shape, shards, -0.22, 0.18) * values
    return jnp.clip(values, min=-bound, max=bound).astype(kind)


def setup_inputs(seed: int = 0) -> dict:
    keys = jax.random.split(jax.random.key(seed), 7)
    start_states = gaussian(keys[0], (SLICES, NR, NA, NZ), 1.0, 6.0, ((0, 32), (1, 4), (2, 2)), jnp.float32)
    target = gaussian(keys[1], (SLICES, NR, NA, NZ), 1.0, 6.0, ((0, 32), (1, 4), (2, 2)), jnp.float32)
    conductivity = jnp.clip(jnp.exp(math.log(1000.0) - 9.2103404 * jax.random.uniform(keys[2], (NR, NA, NZ), jnp.float32) ** block_scale(keys[2], (NR, NA, NZ), ((0, 4), (1, 2)), -0.2, 0.2)), 0.1, 1000.0)
    material = set_ends(jax.random.randint(keys[3], (NR, NA, NZ), 0, 3), jax.random.fold_in(keys[3], 1), 0, 2).astype(jnp.int32)
    current = gaussian(keys[4], (NR, NA, NZ), 1.0, 6.0, ((0, 4), (1, 2)), jnp.float32)
    bh_coef = jnp.clip(jax.random.uniform(keys[5], (3,), jnp.float32, 0.05, 0.5), 0.05, 0.5)
    return {"start_states": start_states, "target": target, "conductivity": conductivity, "material": material, "current": current, "bh_coef": bh_coef}


DT_FINE = 0.25
LOWER_EDGE = 0.05
UPPER_EDGE = 1.95


def square_field(extended):
    radial = 0.5 * (extended[2:, 1:-1] - extended[:-2, 1:-1])
    azimuthal = 0.5 * (extended[1:-1, 2:] - extended[1:-1, :-2])
    return radial * radial + azimuthal * azimuthal


def reluctance(bsquare, mat_ext, bh_coef):
    saturation = bsquare / (1.0 + bsquare)
    iron_value = bh_coef[2] + bh_coef[0] * jnp.exp(bh_coef[1] * saturation)
    return jnp.where(mat_ext == 1, iron_value, 1.0), saturation


def face_terms(reluct_ext):
    centre = reluct_ext[1:-1, 1:-1]
    axial = jnp.pad(centre, ((0, 0), (0, 0), (1, 1)), constant_values=1.0)
    return (0.5 * (centre + reluct_ext[2:, 1:-1]), 0.5 * (centre + reluct_ext[:-2, 1:-1]),
            0.5 * (centre + reluct_ext[1:-1, 2:]), 0.5 * (centre + reluct_ext[1:-1, :-2]),
            0.5 * (centre + axial[:, :, 2:]), 0.5 * (centre + axial[:, :, :-2]))


def apply_operator(extended, face_list, mass_term):
    centre = extended[1:-1, 1:-1]
    axial = jnp.pad(centre, ((0, 0), (0, 0), (1, 1)))
    neighbours = (extended[2:, 1:-1], extended[:-2, 1:-1], extended[1:-1, 2:],
                  extended[1:-1, :-2], axial[:, :, 2:], axial[:, :, :-2])
    result = mass_term * centre
    for face, beside in zip(face_list, neighbours):
        result = result + face * (centre - beside)
    return result


def implicit_step(start_field, extended, mat_ext, mass_term, forcing, bh_coef, widen):
    reluct_ext, saturation = reluctance(square_field(extended), mat_ext, bh_coef)
    face_list = face_terms(reluct_ext)
    diagonal = mass_term
    for face in face_list:
        diagonal = diagonal + face
    inverse = 1.0 / diagonal
    theta = 0.5 * (UPPER_EDGE + LOWER_EDGE)
    delta = 0.5 * (UPPER_EDGE - LOWER_EDGE)
    scaled = theta / delta
    ratio = 1.0 / scaled
    residual = mass_term * start_field + forcing - apply_operator(extended[1:-1, 1:-1], face_list, mass_term)
    direction = residual * inverse / theta
    iterate = start_field
    for sweep_index in range(SWEEPS):
        iterate = iterate + direction
        if sweep_index < SWEEPS - 1:
            residual = residual - apply_operator(widen(direction), face_list, mass_term)
            following = 1.0 / (2.0 * scaled - ratio)
            direction = following * ratio * direction + (2.0 * following / delta) * residual * inverse
            ratio = following
    return iterate, reluct_ext[1:-1, 1:-1], saturation[1:-1, 1:-1]


def coarse_factor(conductivity, reluct_zero, dt_coarse):
    lumped = 6.0 * reluct_zero
    return conductivity / (conductivity + dt_coarse * lumped), lumped


def gradient_terms(slope, jump, conductivity, lumped, dt_coarse, iron, saturation, bh_coef):
    weight = slope * jump
    denom = conductivity + dt_coarse * lumped
    denom_sq = denom * denom
    grad_cond = weight * (dt_coarse * lumped) / denom_sq
    hterm = 6.0 * weight * (-dt_coarse * conductivity) / denom_sq * iron
    growth = jnp.exp(bh_coef[1] * saturation)
    coef_part = jnp.stack([jnp.sum(hterm * growth), jnp.sum(hterm * bh_coef[0] * saturation * growth), jnp.sum(hterm)])
    return grad_cond, coef_part


def widen_one(values):
    return jnp.pad(values, ((1, 1), (1, 1), (0, 0)))


def widen_two(values):
    return jnp.pad(values, ((2, 2), (2, 2), (0, 0)))


def reference(start_states, target, conductivity, material, current, bh_coef):
    mass_term = conductivity / DT_FINE
    mat_ext = jnp.pad(material, ((1, 1), (1, 1), (0, 0)))
    source = current * (material == 2).astype(jnp.float32)
    iron = (material == 1).astype(jnp.float32)
    angular = 4.0 * math.pi / (SLICES * STEPS)
    dt_coarse = STEPS * DT_FINE

    def forward(begin, inputs):
        old_start, target_field, slice_pos = inputs
        current_field = old_start
        reluct_zero = None
        saturation_zero = None
        for step_index in range(STEPS):
            extended = widen_two(current_field)
            forcing = source * jnp.cos(angular * (slice_pos * STEPS + (step_index + 1)))
            current_field, reluct_now, saturation_now = implicit_step(current_field, extended, mat_ext, mass_term, forcing, bh_coef, widen_one)
            if step_index == 0:
                reluct_zero = reluct_now
                saturation_zero = saturation_now
        factor, lumped = coarse_factor(conductivity, reluct_zero, dt_coarse)
        jump = begin - old_start
        end_field = current_field + factor * jump
        resid = end_field - target_field
        return end_field, (end_field, factor, lumped, jump, resid, saturation_zero)

    positions = jnp.arange(SLICES).astype(jnp.float32)
    unused, stacked = lax.scan(forward, start_states[0], (start_states, target, positions))
    end_all, factor_all, lumped_all, jump_all, resid_all, saturation_all = stacked

    def backward(carry, inputs):
        tail, grad_total, coef_total = carry
        resid, factor, lumped, jump, saturation = inputs
        slope = resid + tail
        grad_cond, coef_part = gradient_terms(slope, jump, conductivity, lumped, dt_coarse, iron, saturation, bh_coef)
        return (factor * slope, grad_total + grad_cond, coef_total + coef_part), None

    start_carry = (jnp.zeros_like(conductivity), jnp.zeros_like(conductivity), jnp.zeros((3,), jnp.float32))
    final, unused_out = lax.scan(backward, start_carry, (resid_all, factor_all, lumped_all, jump_all, saturation_all), reverse=True)
    count = SLICES * NR * NA * NZ
    return end_all, final[1], final[2] / count
```

```python
import functools
import math

import jax
import jax.numpy as jnp
from jax import lax
from jax.experimental import pallas as pl
from jax.experimental.pallas import tpu as pltpu
from jax.sharding import PartitionSpec as P

STEPS = 2
SWEEPS = 8
DT_FINE = 0.25
LOWER_EDGE = 0.05
UPPER_EDGE = 1.95

BLOCKS = 8
RADS = 4
RB = 16
AB = 16
NZ = 128
ZB = NZ // BLOCKS
HALO = 2 * SWEEPS
WIN = ZB + 2 * HALO
SLICES = 32
GROUP = 2 * WIN
FIELDS = 4
ROWS = FIELDS * GROUP + 2 * ZB
PAD = 8
HALF = RB // 2
VMEM = 48 * 1024 * 1024


def lane_groups(tiles):
    tiles = list(tiles)
    lane = lax.broadcasted_iota(jnp.int32, tiles[0].shape, 1)
    for bit in (4, 2, 1):
        low = (lane & (16 * bit)) == 0
        for i in range(8):
            if i & bit:
                continue
            first, second = tiles[i], tiles[i + bit]
            tiles[i] = jnp.where(low, first, pltpu.roll(second, 16 * bit, 1))
            tiles[i + bit] = jnp.where(low, pltpu.roll(first, 128 - 16 * bit, 1), second)
    return tiles


def block_of(group):
    return (group % 2) * RADS + group // 2


def pack_kernel(start, target, cond, material, current, out):
    def turned(values):
        return jnp.transpose(values.reshape(HALF * AB, NZ))

    for half in range(2):
        own = pl.ds(half * HALF, HALF)
        mat = material[own]
        iron = jnp.where(mat == 1, 1.0, 0.0)
        source = jnp.where(mat == 2, current[own], 0.0)
        for field, values in enumerate((start[own], iron, cond[own], source)):
            flat = turned(values)
            padded = jnp.concatenate(
                [jnp.zeros((HALO, NZ), jnp.float32), flat, jnp.zeros((HALO, NZ), jnp.float32)], axis=0
            )
            for j in range(BLOCKS):
                out[pl.ds(j * ROWS + field * GROUP + half * WIN, WIN), :] = padded[ZB * j : ZB * j + WIN]
        flat = turned(target[own])
        for j in range(BLOCKS):
            out[pl.ds(j * ROWS + FIELDS * GROUP + half * ZB, ZB), :] = flat[ZB * j : ZB * (j + 1)]


def fine_kernel(coef, got, out, static, x, rho, iron, cond, source, sat, step_d, base, a_rp, a_rm, a_ap, a_am, a_zp, a_zm):
    b0, b1, b2 = coef[0], coef[1], coef[2]
    me = lax.axis_index("azi") * RADS + lax.axis_index("rad")
    slot = lax.axis_index("tm")

    def spread(field, dest, lift):
        for half in range(2):
            for tile in range(WIN // 8):
                rows = field * GROUP + half * WIN + tile * 8
                tiles = [got[pl.ds(block_of(g) * ROWS + rows, 8), :] for g in range(8)]
                for g, value in enumerate(lane_groups(tiles)):
                    dest(half * HALF + g, tile * 8, value)

    def to_x(i, row, value):
        x[0, i + 1, pl.ds(PAD + row, 8), :] = value

    def to(ref):
        def put(i, row, value):
            ref[i, pl.ds(row, 8), :] = value

        return put

    spread(0, to_x, PAD)
    spread(1, to(iron), 0)
    spread(2, to(cond), 0)
    spread(3, to(source), 0)

    blank = jnp.zeros((PAD, NZ), jnp.float32)
    for i in range(RB + 2):
        for buf in range(2):
            x[buf, i, pl.ds(0, PAD), :] = blank
            x[buf, i, pl.ds(PAD + WIN, PAD), :] = blank
        rho[i, pl.ds(0, PAD), :] = blank + 1.0
        rho[i, pl.ds(PAD + WIN, PAD), :] = blank + 1.0

    def wrap(ref_get, ref_put, size, outside):
        lane = lax.broadcasted_iota(jnp.int32, (size, NZ), 1)
        ref_put(0, jnp.where(lane < 32, outside, pltpu.roll(ref_get(RB), 32, 1)))
        ref_put(RB + 1, jnp.where(lane >= 96, outside, pltpu.roll(ref_get(1), 96, 1)))

    def wrap_x(buf, z0, nz):
        rows = pl.ds(PAD + z0, nz)

        def put(i, value):
            x[buf, i, rows, :] = value

        wrap(lambda i: x[buf, i, rows, :], put, nz, 0.0)

    def wrap_rho(z0, nz):
        rows = pl.ds(PAD + z0, nz)

        def put(i, value):
            rho[i, rows, :] = value

        wrap(lambda i: rho[i, rows, :], put, nz, 1.0)

    def prepare(buf, step, z0, nz):
        lane = lax.broadcasted_iota(jnp.int32, (nz, NZ), 1) & 31
        row = lax.broadcasted_iota(jnp.int32, (nz, NZ), 0) + (z0 - HALO) + me * ZB
        first, last = lane == 0, lane == 31
        rows = pl.ds(PAD + z0, nz)
        own = pl.ds(z0, nz)

        def curve(i, carry):
            u = x[buf, i + 1, rows, :]
            radial = 0.5 * (x[buf, i + 2, rows, :] - x[buf, i, rows, :])
            after = jnp.where(last, 0.0, pltpu.roll(u, NZ - 1, 1))
            before = jnp.where(first, 0.0, pltpu.roll(u, 1, 1))
            azimuthal = 0.5 * (after - before)
            square = radial * radial + azimuthal * azimuthal
            saturation = square / (1.0 + square)
            value = b2 + b0 * jnp.exp(b1 * saturation)
            rho[i + 1, rows, :] = jnp.where(iron[i, own, :] > 0.5, value, 1.0)
            if step == 0:
                sat[i] = saturation[HALO - z0 : HALO - z0 + ZB]
            return carry

        lax.fori_loop(0, RB, curve, 0)
        wrap_rho(z0, nz)
        angle = (4.0 * math.pi / (SLICES * STEPS)) * (slot * STEPS + (step + 1)).astype(jnp.float32)
        wave = jnp.cos(jnp.full((8, NZ), angle, jnp.float32))[0:1]

        def faces(i, carry):
            centre = rho[i + 1, rows, :]
            rp = 0.5 * (centre + rho[i + 2, rows, :])
            rm = 0.5 * (centre + rho[i, rows, :])
            ap = 0.5 * (centre + jnp.where(last, 1.0, pltpu.roll(centre, NZ - 1, 1)))
            am = 0.5 * (centre + jnp.where(first, 1.0, pltpu.roll(centre, 1, 1)))
            zp = 0.5 * (centre + rho[i + 1, pl.ds(PAD + z0 + 1, nz), :])
            zm = 0.5 * (centre + rho[i + 1, pl.ds(PAD + z0 - 1, nz), :])
            mass = cond[i, own, :] * (1.0 / DT_FINE)
            inverse = 1.0 / (mass + rp + rm + ap + am + zp + zm)
            a_rp[i, own, :] = inverse * rp
            a_rm[i, own, :] = inverse * rm
            a_ap[i, own, :] = jnp.where(last, 0.0, inverse * ap)
            a_am[i, own, :] = jnp.where(first, 0.0, inverse * am)
            a_zp[i, own, :] = jnp.where(row == NZ - 1, 0.0, inverse * zp)
            a_zm[i, own, :] = jnp.where(row == 0, 0.0, inverse * zm)
            base[i, own, :] = inverse * (mass * x[buf, i + 1, rows, :] + wave * source[i, own, :])
            return carry

        lax.fori_loop(0, RB, faces, 0)

    def sweep(buf, alpha, beta, z0, nz, wrapped):
        rows = pl.ds(PAD + z0, nz)
        own = pl.ds(z0, nz)

        def body(i, carry):
            centre = x[buf, i + 1, rows, :]
            total = base[i, own, :] - centre
            total = total + a_rp[i, own, :] * x[buf, i + 2, rows, :]
            total = total + a_rm[i, own, :] * x[buf, i, rows, :]
            total = total + a_ap[i, own, :] * pltpu.roll(centre, NZ - 1, 1)
            total = total + a_am[i, own, :] * pltpu.roll(centre, 1, 1)
            total = total + a_zp[i, own, :] * x[buf, i + 1, pl.ds(PAD + z0 + 1, nz), :]
            total = total + a_zm[i, own, :] * x[buf, i + 1, pl.ds(PAD + z0 - 1, nz), :]
            change = beta * total
            if alpha is not None:
                change = change + alpha * step_d[i, own, :]
            if wrapped:
                step_d[i, own, :] = change
            x[1 - buf, i + 1, rows, :] = centre + change
            return carry

        lax.fori_loop(0, RB, body, 0, unroll=2)

    theta = 0.5 * (UPPER_EDGE + LOWER_EDGE)
    delta = 0.5 * (UPPER_EDGE - LOWER_EDGE)
    scaled = theta / delta
    buf = 0
    wrap_x(0, 0, WIN)
    for step in range(STEPS):
        z0 = step * SWEEPS
        nz = WIN - 2 * z0
        prepare(buf, step, z0, nz)
        ratio = 1.0 / scaled
        alpha, beta = None, 1.0 / theta
        for index in range(SWEEPS):
            final = index == SWEEPS - 1
            if final:
                z0, nz = z0 + SWEEPS, nz - 2 * SWEEPS
            sweep(buf, alpha, beta, z0, nz, not final)
            buf = 1 - buf
            if not (final and step == STEPS - 1):
                wrap_x(buf, z0, nz)
            following = 1.0 / (2.0 * scaled - ratio)
            alpha, beta = following * ratio, 2.0 * following / delta
            ratio = following

    def put(kind, half, tile, block, value):
        out[pl.ds(((half * ZB + tile * 8) * 4 + kind) * 8 + block, 8, stride=32), :] = value

    for half in range(2):
        for tile in range(ZB // 8):
            ends = [x[buf, half * HALF + g + 1, pl.ds(PAD + HALO + tile * 8, 8), :] for g in range(8)]
            for g, value in enumerate(lane_groups(ends)):
                put(0, half, tile, block_of(g), value)
            sats = [sat[half * HALF + g, pl.ds(tile * 8, 8), :] for g in range(8)]
            for g, value in enumerate(lane_groups(sats)):
                put(1, half, tile, block_of(g), value)
            for block in range(BLOCKS):
                rows = block * ROWS + half * WIN + HALO + tile * 8
                put(2, half, tile, block, got[pl.ds(rows, 8), :])
                rows = block * ROWS + FIELDS * GROUP + half * ZB + tile * 8
                put(3, half, tile, block, got[pl.ds(rows, 8), :])

    place = (slot // ZB) * WIN + HALO + slot % ZB
    static[pl.ds(0, 8), :] = got[pl.ds(2 * GROUP + place, 8, stride=ROWS), :]
    static[pl.ds(8, 8), :] = got[pl.ds(1 * GROUP + place, 8, stride=ROWS), :]


def chain_kernel(coef, got, static, out, jumps, resids, factors, quads):
    b0, b1, b2 = coef[0], coef[1], coef[2]
    cond = static[pl.ds(0, 8), :]
    iron = static[pl.ds(8, 8), :]
    is_iron = iron > 0.5
    dt = STEPS * DT_FINE

    def part(n, kind):
        return got[pl.ds(n * 32 + kind * 8, 8), :]

    jump = jnp.zeros((8, NZ), jnp.float32)
    for n in range(SLICES):
        growth = jnp.exp(b1 * part(n, 1))
        lumped = 6.0 * jnp.where(is_iron, b2 + b0 * growth, 1.0)
        inverse = 1.0 / (cond + dt * lumped)
        factor = cond * inverse
        end = part(n, 0) + factor * jump
        out[pl.ds(n * 32, 8, stride=4), :] = end
        jumps[n] = jump
        resids[n] = end - part(n, 3)
        factors[n] = factor
        quads[n] = inverse * inverse
        if n < SLICES - 1:
            jump = end - part(n + 1, 2)

    tail = jnp.zeros((8, NZ), jnp.float32)
    grad = jnp.zeros((8, NZ), jnp.float32)
    sums = [jnp.zeros((8, NZ), jnp.float32) for _ in range(3)]
    for n in reversed(range(SLICES)):
        saturation = part(n, 1)
        growth = jnp.exp(b1 * saturation)
        lumped = 6.0 * jnp.where(is_iron, b2 + b0 * growth, 1.0)
        slope = resids[n] + tail
        scaled = slope * jumps[n] * quads[n]
        grad = grad + scaled * (dt * lumped)
        hterm = (6.0 * scaled) * (-dt * cond) * iron
        grown = hterm * growth
        sums[0] = sums[0] + grown
        sums[1] = sums[1] + grown * (b0 * saturation)
        sums[2] = sums[2] + hterm
        tail = factors[n] * slope
    lane = lax.broadcasted_iota(jnp.int32, (8, NZ), 1)
    totals = [jnp.sum(value, keepdims=True) for value in sums]
    row = jnp.where(lane == 0, totals[0], jnp.where(lane == 1, totals[1], jnp.where(lane == 2, totals[2], 0.0)))
    for n in range(SLICES):
        out[pl.ds(n * 32 + 1, 8, stride=4), :] = grad
        out[pl.ds(n * 32 + 2, 8, stride=4), :] = row
        out[pl.ds(n * 32 + 3, 8, stride=4), :] = row


def unpack_kernel(got, end, grad, coef_grad):
    for kind, dest in enumerate((end, grad)):
        for half in range(2):
            flat = jnp.concatenate(
                [got[pl.ds(half * ZB * 32 + j * 4 + kind, ZB, stride=32), :] for j in range(BLOCKS)], axis=0
            )
            dest[pl.ds(half * HALF, HALF)] = jnp.transpose(flat).reshape(HALF, AB, NZ)
    sums = jnp.sum(got[pl.ds(2, SLICES * BLOCKS, stride=4), :], axis=0, keepdims=True)
    lane = lax.broadcasted_iota(jnp.int32, (1, NZ), 1)
    count = SLICES * BLOCKS * RB * AB * NZ
    for c in range(3):
        coef_grad[c] = jnp.sum(jnp.where(lane == c, sums, 0.0)) * (1.0 / count)


def vmem():
    return pl.BlockSpec(memory_space=pltpu.VMEM)


def smem():
    return pl.BlockSpec(memory_space=pltpu.SMEM)


def call(kernel, outs, ins, scratch, out_specs=None):
    specs = [smem() if place == "s" else vmem() for place in ins]
    return pl.pallas_call(
        kernel,
        out_shape=outs,
        in_specs=specs,
        out_specs=out_specs if out_specs is not None else jax.tree.map(lambda leaf: vmem(), outs),
        scratch_shapes=scratch,
        compiler_params=pltpu.CompilerParams(vmem_limit_bytes=VMEM),
    )


def local(start_states, target, conductivity, material, current, bh_coef):
    def shape(*dims):
        return jax.ShapeDtypeStruct(dims, jnp.float32)

    packed = call(pack_kernel, shape(BLOCKS * ROWS, NZ), "vvvvv", [])(
        start_states[0], target[0], conductivity, material, current
    )
    whole = lax.all_to_all(packed, ("azi", "rad"), 0, 0, tiled=True)
    block = pltpu.VMEM((RB, WIN, NZ), jnp.float32)
    fine, static = call(
        fine_kernel,
        (shape(SLICES * 32, NZ), shape(16, NZ)),
        "sv",
        [
            pltpu.VMEM((2, RB + 2, WIN + 2 * PAD, NZ), jnp.float32),
            pltpu.VMEM((RB + 2, WIN + 2 * PAD, NZ), jnp.float32),
            block,
            block,
            block,
            pltpu.VMEM((RB, ZB, NZ), jnp.float32),
        ]
        + [block] * 8,
    )(bh_coef, whole)
    slices = lax.all_to_all(fine, "tm", 0, 0, tiled=True)
    line = pltpu.VMEM((SLICES, 8, NZ), jnp.float32)
    chained = call(chain_kernel, shape(SLICES * 32, NZ), "svv", [line] * 4)(bh_coef, slices, static)
    results = lax.all_to_all(chained, ("tm", "azi", "rad"), 0, 0, tiled=True)
    end, grad, coef_grad = call(
        unpack_kernel,
        (shape(RB, AB, NZ), shape(RB, AB, NZ), shape(3)),
        "v",
        [],
        out_specs=(vmem(), vmem(), smem()),
    )(results)
    return (end[None], grad, coef_grad)


def solution(mesh):
    placed = (
        P("tm", "rad", "azi", None),
        P("tm", "rad", "azi", None),
        P("rad", "azi", None),
        P("rad", "azi", None),
        P("rad", "azi", None),
        P(),
    )
    return jax.shard_map(
        local,
        mesh=mesh,
        in_specs=placed,
        out_specs=(P("tm", "rad", "azi", None), P("rad", "azi", None), P()),
        check_vma=False,
    )
```

```python
import functools
import math

import jax
import jax.numpy as jnp
from jax import lax
from jax.experimental import pallas as pl
from jax.experimental.pallas import tpu as pltpu
from jax.sharding import PartitionSpec as P

STEPS = 2
SWEEPS = 8
DT_FINE = 0.25
LOWER_EDGE = 0.05
UPPER_EDGE = 1.95

BLOCKS = 8
RADS = 4
RB = 16
AB = 16
NZ = 128
ZB = NZ // BLOCKS
HALO = 2 * SWEEPS
WIN = ZB + 2 * HALO
SLICES = 32
GROUP = 2 * WIN
FIELDS = 4
ROWS = FIELDS * GROUP + 2 * ZB
PAD = 8
HALF = RB // 2
VMEM = 48 * 1024 * 1024


def lane_groups(tiles):
    tiles = list(tiles)
    lane = lax.broadcasted_iota(jnp.int32, tiles[0].shape, 1)
    for bit in (4, 2, 1):
        low = (lane & (16 * bit)) == 0
        for i in range(8):
            if i & bit:
                continue
            first, second = tiles[i], tiles[i + bit]
            tiles[i] = jnp.where(low, first, pltpu.roll(second, 16 * bit, 1))
            tiles[i + bit] = jnp.where(low, pltpu.roll(first, 128 - 16 * bit, 1), second)
    return tiles


def block_of(group):
    return (group % 2) * RADS + group // 2


def pack_kernel(start_at, target_at, cond_at, material_at, current_at, out, start, target, cond, material, current, sems):
    pairs = ((start_at, start), (material_at, material), (cond_at, cond), (current_at, current), (target_at, target))
    copies = [pltpu.make_async_copy(src, dst, sems.at[k]) for k, (src, dst) in enumerate(pairs)]
    for copy in copies:
        copy.start()

    def turned(values):
        return jnp.transpose(values.reshape(HALF * AB, NZ))

    def put(field, half, values):
        edge = jnp.zeros((HALO, NZ), jnp.float32)
        padded = jnp.concatenate([edge, turned(values), edge], axis=0)
        for j in range(BLOCKS):
            out[pl.ds(j * ROWS + field * GROUP + half * WIN, WIN), :] = padded[ZB * j : ZB * j + WIN]

    halves = [pl.ds(half * HALF, HALF) for half in range(2)]
    copies[0].wait()
    for half in range(2):
        put(0, half, start[halves[half]])
    copies[1].wait()
    for half in range(2):
        put(1, half, jnp.where(material[halves[half]] == 1, 1.0, 0.0))
    copies[2].wait()
    for half in range(2):
        put(2, half, cond[halves[half]])
    copies[3].wait()
    for half in range(2):
        put(3, half, jnp.where(material[halves[half]] == 2, current[halves[half]], 0.0))
    copies[4].wait()
    for half in range(2):
        flat = turned(target[halves[half]])
        for j in range(BLOCKS):
            out[pl.ds(j * ROWS + FIELDS * GROUP + half * ZB, ZB), :] = flat[ZB * j : ZB * (j + 1)]


def fine_kernel(coef, got, out, static, xa, xb, rho, iron, cond, source, sat, step_d, base, a_rp, a_rm, a_ap, a_am, a_zp, a_zm):
    b0, b1, b2 = coef[0], coef[1], coef[2]
    me = lax.axis_index("azi") * RADS + lax.axis_index("rad")
    slot = lax.axis_index("tm")

    def spread(field, dest, lift):
        for half in range(2):
            for tile in range(WIN // 8):
                rows = field * GROUP + half * WIN + tile * 8
                tiles = [got[pl.ds(block_of(g) * ROWS + rows, 8), :] for g in range(8)]
                for g, value in enumerate(lane_groups(tiles)):
                    dest(half * HALF + g, tile * 8, value)

    def to_x(i, row, value):
        xa[i + 1, pl.ds(PAD + row, 8), :] = value

    def to(ref):
        def put(i, row, value):
            ref[i, pl.ds(row, 8), :] = value

        return put

    def some(tile, carry):
        row = pl.multiple_of(tile * 8, 8)
        for field, dest in ((0, to_x), (1, to(iron)), (2, to(cond)), (3, to(source))):
            for half in range(2):
                rows = field * GROUP + half * WIN + row
                tiles = [got[pl.ds(pl.multiple_of(block_of(g) * ROWS + rows, 8), 8), :] for g in range(8)]
                for g, value in enumerate(lane_groups(tiles)):
                    dest(half * HALF + g, row, value)
        return carry

    lax.fori_loop(0, WIN // 8, some, 0)

    blank = jnp.zeros((PAD, NZ), jnp.float32)
    for i in range(RB + 2):
        for x in (xa, xb):
            x[i, pl.ds(0, PAD), :] = blank
            x[i, pl.ds(PAD + WIN, PAD), :] = blank
        rho[i, pl.ds(0, PAD), :] = blank + 1.0
        rho[i, pl.ds(PAD + WIN, PAD), :] = blank + 1.0

    def wrap(ref_get, ref_put, size, outside):
        lane = lax.broadcasted_iota(jnp.int32, (size, NZ), 1)
        ref_put(0, jnp.where(lane < 32, outside, pltpu.roll(ref_get(RB), 32, 1)))
        ref_put(RB + 1, jnp.where(lane >= 96, outside, pltpu.roll(ref_get(1), 96, 1)))

    def wrap_x(x, z0, nz):
        rows = pl.ds(PAD + z0, nz)

        def put(i, value):
            x[i, rows, :] = value

        wrap(lambda i: x[i, rows, :], put, nz, 0.0)

    def wrap_rho(z0, nz):
        rows = pl.ds(PAD + z0, nz)

        def put(i, value):
            rho[i, rows, :] = value

        wrap(lambda i: rho[i, rows, :], put, nz, 1.0)

    def prepare(x, step, z0, nz):
        lane = lax.broadcasted_iota(jnp.int32, (nz, NZ), 1) & 31
        row = lax.broadcasted_iota(jnp.int32, (nz, NZ), 0) + (z0 - HALO) + me * ZB
        first, last = lane == 0, lane == 31
        rows = pl.ds(PAD + z0, nz)
        own = pl.ds(z0, nz)

        def curve(i, carry):
            u = x[i + 1, rows, :]
            radial = 0.5 * (x[i + 2, rows, :] - x[i, rows, :])
            after = jnp.where(last, 0.0, pltpu.roll(u, NZ - 1, 1))
            before = jnp.where(first, 0.0, pltpu.roll(u, 1, 1))
            azimuthal = 0.5 * (after - before)
            square = radial * radial + azimuthal * azimuthal
            saturation = square / (1.0 + square)
            value = b2 + b0 * jnp.exp(b1 * saturation)
            rho[i + 1, rows, :] = jnp.where(iron[i, own, :] > 0.5, value, 1.0)
            if step == 0:
                sat[i] = saturation[HALO - z0 : HALO - z0 + ZB]
            return carry

        for i in range(RB):
            curve(i, 0)
        wrap_rho(z0, nz)
        angle = (4.0 * math.pi / (SLICES * STEPS)) * (slot * STEPS + (step + 1)).astype(jnp.float32)
        wave = jnp.cos(jnp.full((8, NZ), angle, jnp.float32))[0:1]

        def faces(i, carry):
            centre = rho[i + 1, rows, :]
            rp = 0.5 * (centre + rho[i + 2, rows, :])
            rm = 0.5 * (centre + rho[i, rows, :])
            ap = 0.5 * (centre + jnp.where(last, 1.0, pltpu.roll(centre, NZ - 1, 1)))
            am = 0.5 * (centre + jnp.where(first, 1.0, pltpu.roll(centre, 1, 1)))
            zp = 0.5 * (centre + rho[i + 1, pl.ds(PAD + z0 + 1, nz), :])
            zm = 0.5 * (centre + rho[i + 1, pl.ds(PAD + z0 - 1, nz), :])
            mass = cond[i, own, :] * (1.0 / DT_FINE)
            inverse = 1.0 / (mass + rp + rm + ap + am + zp + zm)
            a_rp[i, own, :] = inverse * rp
            a_rm[i, own, :] = inverse * rm
            a_ap[i, own, :] = jnp.where(last, 0.0, inverse * ap)
            a_am[i, own, :] = jnp.where(first, 0.0, inverse * am)
            a_zp[i, own, :] = jnp.where(row == NZ - 1, 0.0, inverse * zp)
            a_zm[i, own, :] = jnp.where(row == 0, 0.0, inverse * zm)
            base[i, own, :] = inverse * (mass * x[i + 1, rows, :] + wave * source[i, own, :])
            return carry

        for i in range(RB):
            faces(i, 0)

    def sweep(x, fresh, alpha, beta, z0, nz, final):
        rows = pl.ds(PAD + z0, nz)
        own = pl.ds(z0, nz)
        lane = lax.broadcasted_iota(jnp.int32, (nz, NZ), 1)
        for i in range(RB):
            centre = x[i + 1, rows, :]
            total = base[i, own, :] - centre
            total = total + a_rp[i, own, :] * x[i + 2, rows, :]
            total = total + a_rm[i, own, :] * x[i, rows, :]
            total = total + a_ap[i, own, :] * pltpu.roll(centre, NZ - 1, 1)
            total = total + a_am[i, own, :] * pltpu.roll(centre, 1, 1)
            total = total + a_zp[i, own, :] * x[i + 1, pl.ds(PAD + z0 + 1, nz), :]
            total = total + a_zm[i, own, :] * x[i + 1, pl.ds(PAD + z0 - 1, nz), :]
            change = beta * total
            if alpha is not None:
                change = change + alpha * step_d[i, own, :]
            if not final:
                step_d[i, own, :] = change
            value = centre + change
            fresh[i + 1, rows, :] = value
            if i == 0:
                fresh[RB + 1, rows, :] = jnp.where(lane >= 96, 0.0, pltpu.roll(value, 96, 1))
            if i == RB - 1:
                fresh[0, rows, :] = jnp.where(lane < 32, 0.0, pltpu.roll(value, 32, 1))

    theta = 0.5 * (UPPER_EDGE + LOWER_EDGE)
    delta = 0.5 * (UPPER_EDGE - LOWER_EDGE)
    scaled = theta / delta
    ratio, alphas, betas = 1.0 / scaled, [0.0], [1.0 / theta]
    for index in range(SWEEPS - 1):
        following = 1.0 / (2.0 * scaled - ratio)
        alphas.append(following * ratio)
        betas.append(2.0 * following / delta)
        ratio = following

    def pick(values, first, at):
        chosen = jnp.float32(values[first])
        for k in range(1, (SWEEPS - first) // 2):
            chosen = jnp.where(at == k, jnp.float32(values[first + 2 * k]), chosen)
        return chosen

    wrap_x(xa, 0, WIN)
    for step in range(STEPS):
        z0 = step * SWEEPS
        nz = WIN - 2 * z0
        prepare(xa, step, z0, nz)
        sweep(xa, xb, None, betas[0], z0, nz, False)

        def pair(at, carry):
            sweep(xb, xa, pick(alphas, 1, at), pick(betas, 1, at), z0, nz, False)
            sweep(xa, xb, pick(alphas, 2, at), pick(betas, 2, at), z0, nz, False)
            return carry

        lax.fori_loop(0, (SWEEPS - 2) // 2, pair, 0)
        sweep(xb, xa, alphas[-1], betas[-1], z0 + SWEEPS, nz - 2 * SWEEPS, True)

    def put(kind, half, tile, block, value):
        out[pl.ds(((half * ZB + tile * 8) * 4 + kind) * 8 + block, 8, stride=32), :] = value

    for half in range(2):
        for tile in range(ZB // 8):
            ends = [xa[half * HALF + g + 1, pl.ds(PAD + HALO + tile * 8, 8), :] for g in range(8)]
            for g, value in enumerate(lane_groups(ends)):
                put(0, half, tile, block_of(g), value)
            sats = [sat[half * HALF + g, pl.ds(tile * 8, 8), :] for g in range(8)]
            for g, value in enumerate(lane_groups(sats)):
                put(1, half, tile, block_of(g), value)
            for block in range(BLOCKS):
                rows = block * ROWS + half * WIN + HALO + tile * 8
                put(2, half, tile, block, got[pl.ds(rows, 8), :])
                rows = block * ROWS + FIELDS * GROUP + half * ZB + tile * 8
                put(3, half, tile, block, got[pl.ds(rows, 8), :])

    place = (slot // ZB) * WIN + HALO + slot % ZB
    static[pl.ds(0, 8), :] = got[pl.ds(2 * GROUP + place, 8, stride=ROWS), :]
    static[pl.ds(8, 8), :] = got[pl.ds(1 * GROUP + place, 8, stride=ROWS), :]


def chain_kernel(coef, got, static, out, jumps, resids, factors, quads):
    b0, b1, b2 = coef[0], coef[1], coef[2]
    cond = static[pl.ds(0, 8), :]
    iron = static[pl.ds(8, 8), :]
    is_iron = iron > 0.5
    dt = STEPS * DT_FINE

    def part(n, kind):
        return got[pl.ds(n * 32 + kind * 8, 8), :]

    jump = jnp.zeros((8, NZ), jnp.float32)
    for n in range(SLICES):
        growth = jnp.exp(b1 * part(n, 1))
        lumped = 6.0 * jnp.where(is_iron, b2 + b0 * growth, 1.0)
        inverse = 1.0 / (cond + dt * lumped)
        factor = cond * inverse
        end = part(n, 0) + factor * jump
        out[pl.ds(n * 24, 8, stride=3), :] = end
        jumps[n] = jump
        resids[n] = end - part(n, 3)
        factors[n] = factor
        quads[n] = inverse * inverse
        if n < SLICES - 1:
            jump = end - part(n + 1, 2)

    tail = jnp.zeros((8, NZ), jnp.float32)
    grad = jnp.zeros((8, NZ), jnp.float32)
    sums = [jnp.zeros((8, NZ), jnp.float32) for _ in range(3)]
    for n in reversed(range(SLICES)):
        saturation = part(n, 1)
        growth = jnp.exp(b1 * saturation)
        lumped = 6.0 * jnp.where(is_iron, b2 + b0 * growth, 1.0)
        slope = resids[n] + tail
        scaled = slope * jumps[n] * quads[n]
        grad = grad + scaled * (dt * lumped)
        hterm = (6.0 * scaled) * (-dt * cond) * iron
        grown = hterm * growth
        sums[0] = sums[0] + grown
        sums[1] = sums[1] + grown * (b0 * saturation)
        sums[2] = sums[2] + hterm
        tail = factors[n] * slope
    lane = lax.broadcasted_iota(jnp.int32, (8, NZ), 1)
    totals = [jnp.sum(value, keepdims=True) for value in sums]
    row = jnp.where(lane == 0, totals[0], jnp.where(lane == 1, totals[1], jnp.where(lane == 2, totals[2], 0.0)))
    for n in range(SLICES):
        out[pl.ds(n * 24 + 1, 8, stride=3), :] = grad
        out[pl.ds(n * 24 + 2, 8, stride=3), :] = row


def unpack_kernel(got, end, grad, coef_grad):
    for kind, dest in enumerate((end, grad)):
        for half in range(2):
            flat = jnp.concatenate(
                [got[pl.ds(half * ZB * 24 + j * 3 + kind, ZB, stride=24), :] for j in range(BLOCKS)], axis=0
            )
            dest[pl.ds(half * HALF, HALF)] = jnp.transpose(flat).reshape(HALF, AB, NZ)
    sums = jnp.sum(got[pl.ds(2, SLICES * BLOCKS, stride=3), :], axis=0, keepdims=True)
    lane = lax.broadcasted_iota(jnp.int32, (1, NZ), 1)
    count = SLICES * BLOCKS * RB * AB * NZ
    for c in range(3):
        coef_grad[c] = jnp.sum(jnp.where(lane == c, sums, 0.0)) * (1.0 / count)


def vmem():
    return pl.BlockSpec(memory_space=pltpu.VMEM)


def smem():
    return pl.BlockSpec(memory_space=pltpu.SMEM)


def call(kernel, outs, ins, scratch, out_specs=None):
    spaces = {"s": pltpu.SMEM, "v": pltpu.VMEM, "a": pltpu.HBM}
    specs = [pl.BlockSpec(memory_space=spaces[place]) for place in ins]
    return pl.pallas_call(
        kernel,
        out_shape=outs,
        in_specs=specs,
        out_specs=out_specs if out_specs is not None else jax.tree.map(lambda leaf: vmem(), outs),
        scratch_shapes=scratch,
        compiler_params=pltpu.CompilerParams(vmem_limit_bytes=VMEM),
    )


def shape(*dims):
    return jax.ShapeDtypeStruct(dims, jnp.float32)


def solve(bh_coef, whole):
    block = pltpu.VMEM((RB, WIN, NZ), jnp.float32)
    return call(
        fine_kernel,
        (shape(SLICES * 32, NZ), shape(16, NZ)),
        "sv",
        [
            pltpu.VMEM((RB + 2, WIN + 2 * PAD, NZ), jnp.float32),
            pltpu.VMEM((RB + 2, WIN + 2 * PAD, NZ), jnp.float32),
            pltpu.VMEM((RB + 2, WIN + 2 * PAD, NZ), jnp.float32),
            block,
            block,
            block,
            pltpu.VMEM((RB, ZB, NZ), jnp.float32),
        ]
        + [block] * 8,
    )(bh_coef, whole)


def local(start_states, target, conductivity, material, current, bh_coef):
    field = pltpu.VMEM((RB, AB, NZ), jnp.float32)
    packed = call(
        pack_kernel,
        shape(BLOCKS * ROWS, NZ),
        "aaaaa",
        [field, field, field, pltpu.VMEM((RB, AB, NZ), jnp.int32), field, pltpu.SemaphoreType.DMA((5,))],
    )(start_states[0], target[0], conductivity, material, current)
    whole = lax.all_to_all(packed, ("azi", "rad"), 0, 0, tiled=True)
    fine, static = solve(bh_coef, whole)
    slices = lax.all_to_all(fine, "tm", 0, 0, tiled=True)
    line = pltpu.VMEM((SLICES, 8, NZ), jnp.float32)
    chained = call(chain_kernel, shape(SLICES * 24, NZ), "svv", [line] * 4)(bh_coef, slices, static)
    results = lax.all_to_all(
        chained.reshape(SLICES * BLOCKS, 1, 3 * NZ), ("tm", "azi", "rad"), 0, 0, tiled=True
    ).reshape(SLICES * 24, NZ)
    end, grad, coef_grad = call(
        unpack_kernel,
        (shape(RB, AB, NZ), shape(RB, AB, NZ), shape(3)),
        "v",
        [],
        out_specs=(vmem(), vmem(), smem()),
    )(results)
    return (end[None], grad, coef_grad)


def solution(mesh):
    placed = (
        P("tm", "rad", "azi", None),
        P("tm", "rad", "azi", None),
        P("rad", "azi", None),
        P("rad", "azi", None),
        P("rad", "azi", None),
        P(),
    )
    return jax.shard_map(
        local,
        mesh=mesh,
        in_specs=placed,
        out_specs=(P("tm", "rad", "azi", None), P("rad", "azi", None), P()),
        check_vma=False,
    )
```

```python
import functools
import math

import jax
import jax.numpy as jnp
from jax import lax
from jax.experimental import pallas as pl
from jax.experimental.pallas import tpu as pltpu
from jax.sharding import PartitionSpec as P

STEPS = 2
SWEEPS = 8
DT_FINE = 0.25
LOWER_EDGE = 0.05
UPPER_EDGE = 1.95

BLOCKS = 8
RADS = 4
RB = 16
AB = 16
NZ = 128
ZB = NZ // BLOCKS
HALO = 2 * SWEEPS
WIN = ZB + 2 * HALO
SLICES = 32
GROUP = 2 * WIN
FIELDS = 4
ROWS = FIELDS * GROUP + 2 * ZB
PAD = 8
HALF = RB // 2
VMEM = 48 * 1024 * 1024
WHOLE_VMEM = 56 * 1024 * 1024


def lane_groups(tiles):
    tiles = list(tiles)
    lane = lax.broadcasted_iota(jnp.int32, tiles[0].shape, 1)
    for bit in (4, 2, 1):
        low = (lane & (16 * bit)) == 0
        for i in range(8):
            if i & bit:
                continue
            first, second = tiles[i], tiles[i + bit]
            tiles[i] = jnp.where(low, first, pltpu.roll(second, 16 * bit, 1))
            tiles[i + bit] = jnp.where(low, pltpu.roll(first, 128 - 16 * bit, 1), second)
    return tiles


def block_of(group):
    return (group % 2) * RADS + group // 2


def pack_kernel(start_at, target_at, cond_at, material_at, current_at, out, start, target, cond, material, current, sems):
    pairs = ((start_at, start), (material_at, material), (cond_at, cond), (current_at, current), (target_at, target))
    copies = [pltpu.make_async_copy(src, dst, sems.at[k]) for k, (src, dst) in enumerate(pairs)]
    for copy in copies:
        copy.start()

    def turned(values):
        return jnp.transpose(values.reshape(HALF * AB, NZ))

    def put(field, half, values):
        edge = jnp.zeros((HALO, NZ), jnp.float32)
        padded = jnp.concatenate([edge, turned(values), edge], axis=0)
        for j in range(BLOCKS):
            out[pl.ds(j * ROWS + field * GROUP + half * WIN, WIN), :] = padded[ZB * j : ZB * j + WIN]

    halves = [pl.ds(half * HALF, HALF) for half in range(2)]
    copies[0].wait()
    for half in range(2):
        put(0, half, start[halves[half]])
    copies[1].wait()
    for half in range(2):
        put(1, half, jnp.where(material[halves[half]] == 1, 1.0, 0.0))
    copies[2].wait()
    for half in range(2):
        put(2, half, cond[halves[half]])
    copies[3].wait()
    for half in range(2):
        put(3, half, jnp.where(material[halves[half]] == 2, current[halves[half]], 0.0))
    copies[4].wait()
    for half in range(2):
        flat = turned(target[halves[half]])
        for j in range(BLOCKS):
            out[pl.ds(j * ROWS + FIELDS * GROUP + half * ZB, ZB), :] = flat[ZB * j : ZB * (j + 1)]


def fine_kernel(coef, got, out, static, xa, xb, rho, iron, cond, source, sat, step_d, base, a_rp, a_rm, a_ap, a_am, a_zp, a_zm):
    b0, b1, b2 = coef[0], coef[1], coef[2]
    me = lax.axis_index("azi") * RADS + lax.axis_index("rad")
    slot = lax.axis_index("tm")

    def spread(field, dest, lift):
        for half in range(2):
            for tile in range(WIN // 8):
                rows = field * GROUP + half * WIN + tile * 8
                tiles = [got[pl.ds(block_of(g) * ROWS + rows, 8), :] for g in range(8)]
                for g, value in enumerate(lane_groups(tiles)):
                    dest(half * HALF + g, tile * 8, value)

    def to_x(i, row, value):
        xa[i + 1, pl.ds(PAD + row, 8), :] = value

    def to(ref):
        def put(i, row, value):
            ref[i, pl.ds(row, 8), :] = value

        return put

    def some(tile, carry):
        row = pl.multiple_of(tile * 8, 8)
        for field, dest in ((0, to_x), (1, to(iron)), (2, to(cond)), (3, to(source))):
            for half in range(2):
                rows = field * GROUP + half * WIN + row
                tiles = [got[pl.ds(pl.multiple_of(block_of(g) * ROWS + rows, 8), 8), :] for g in range(8)]
                for g, value in enumerate(lane_groups(tiles)):
                    dest(half * HALF + g, row, value)
        return carry

    lax.fori_loop(0, WIN // 8, some, 0)

    blank = jnp.zeros((PAD, NZ), jnp.float32)
    for i in range(RB + 2):
        for x in (xa, xb):
            x[i, pl.ds(0, PAD), :] = blank
            x[i, pl.ds(PAD + WIN, PAD), :] = blank
        rho[i, pl.ds(0, PAD), :] = blank + 1.0
        rho[i, pl.ds(PAD + WIN, PAD), :] = blank + 1.0

    def wrap(ref_get, ref_put, size, outside):
        lane = lax.broadcasted_iota(jnp.int32, (size, NZ), 1)
        ref_put(0, jnp.where(lane < 32, outside, pltpu.roll(ref_get(RB), 32, 1)))
        ref_put(RB + 1, jnp.where(lane >= 96, outside, pltpu.roll(ref_get(1), 96, 1)))

    def wrap_x(x, z0, nz):
        rows = pl.ds(PAD + z0, nz)

        def put(i, value):
            x[i, rows, :] = value

        wrap(lambda i: x[i, rows, :], put, nz, 0.0)

    def wrap_rho(z0, nz):
        rows = pl.ds(PAD + z0, nz)

        def put(i, value):
            rho[i, rows, :] = value

        wrap(lambda i: rho[i, rows, :], put, nz, 1.0)

    def prepare(x, step, z0, nz):
        lane = lax.broadcasted_iota(jnp.int32, (nz, NZ), 1) & 31
        row = lax.broadcasted_iota(jnp.int32, (nz, NZ), 0) + (z0 - HALO) + me * ZB
        first, last = lane == 0, lane == 31
        rows = pl.ds(PAD + z0, nz)
        own = pl.ds(z0, nz)

        def curve(i, carry):
            u = x[i + 1, rows, :]
            radial = 0.5 * (x[i + 2, rows, :] - x[i, rows, :])
            after = jnp.where(last, 0.0, pltpu.roll(u, NZ - 1, 1))
            before = jnp.where(first, 0.0, pltpu.roll(u, 1, 1))
            azimuthal = 0.5 * (after - before)
            square = radial * radial + azimuthal * azimuthal
            saturation = square / (1.0 + square)
            value = b2 + b0 * jnp.exp(b1 * saturation)
            rho[i + 1, rows, :] = jnp.where(iron[i, own, :] > 0.5, value, 1.0)
            if step == 0:
                sat[i] = saturation[HALO - z0 : HALO - z0 + ZB]
            return carry

        for i in range(RB):
            curve(i, 0)
        wrap_rho(z0, nz)
        angle = (4.0 * math.pi / (SLICES * STEPS)) * (slot * STEPS + (step + 1)).astype(jnp.float32)
        wave = jnp.cos(jnp.full((8, NZ), angle, jnp.float32))[0:1]

        def faces(i, carry):
            centre = rho[i + 1, rows, :]
            rp = 0.5 * (centre + rho[i + 2, rows, :])
            rm = 0.5 * (centre + rho[i, rows, :])
            ap = 0.5 * (centre + jnp.where(last, 1.0, pltpu.roll(centre, NZ - 1, 1)))
            am = 0.5 * (centre + jnp.where(first, 1.0, pltpu.roll(centre, 1, 1)))
            zp = 0.5 * (centre + rho[i + 1, pl.ds(PAD + z0 + 1, nz), :])
            zm = 0.5 * (centre + rho[i + 1, pl.ds(PAD + z0 - 1, nz), :])
            mass = cond[i, own, :] * (1.0 / DT_FINE)
            inverse = 1.0 / (mass + rp + rm + ap + am + zp + zm)
            a_rp[i, own, :] = inverse * rp
            a_rm[i, own, :] = inverse * rm
            a_ap[i, own, :] = jnp.where(last, 0.0, inverse * ap)
            a_am[i, own, :] = jnp.where(first, 0.0, inverse * am)
            a_zp[i, own, :] = jnp.where(row == NZ - 1, 0.0, inverse * zp)
            a_zm[i, own, :] = jnp.where(row == 0, 0.0, inverse * zm)
            base[i, own, :] = inverse * (mass * x[i + 1, rows, :] + wave * source[i, own, :])
            return carry

        for i in range(RB):
            faces(i, 0)

    def sweep(x, fresh, alpha, beta, z0, nz, final):
        rows = pl.ds(PAD + z0, nz)
        own = pl.ds(z0, nz)
        lane = lax.broadcasted_iota(jnp.int32, (nz, NZ), 1)
        for i in range(RB):
            centre = x[i + 1, rows, :]
            total = base[i, own, :] - centre
            total = total + a_rp[i, own, :] * x[i + 2, rows, :]
            total = total + a_rm[i, own, :] * x[i, rows, :]
            total = total + a_ap[i, own, :] * pltpu.roll(centre, NZ - 1, 1)
            total = total + a_am[i, own, :] * pltpu.roll(centre, 1, 1)
            total = total + a_zp[i, own, :] * x[i + 1, pl.ds(PAD + z0 + 1, nz), :]
            total = total + a_zm[i, own, :] * x[i + 1, pl.ds(PAD + z0 - 1, nz), :]
            change = beta * total
            if alpha is not None:
                change = change + alpha * step_d[i, own, :]
            if not final:
                step_d[i, own, :] = change
            value = centre + change
            fresh[i + 1, rows, :] = value
            if i == 0:
                fresh[RB + 1, rows, :] = jnp.where(lane >= 96, 0.0, pltpu.roll(value, 96, 1))
            if i == RB - 1:
                fresh[0, rows, :] = jnp.where(lane < 32, 0.0, pltpu.roll(value, 32, 1))

    theta = 0.5 * (UPPER_EDGE + LOWER_EDGE)
    delta = 0.5 * (UPPER_EDGE - LOWER_EDGE)
    scaled = theta / delta
    ratio, alphas, betas = 1.0 / scaled, [0.0], [1.0 / theta]
    for index in range(SWEEPS - 1):
        following = 1.0 / (2.0 * scaled - ratio)
        alphas.append(following * ratio)
        betas.append(2.0 * following / delta)
        ratio = following

    def pick(values, first, at):
        chosen = jnp.float32(values[first])
        for k in range(1, (SWEEPS - first) // 2):
            chosen = jnp.where(at == k, jnp.float32(values[first + 2 * k]), chosen)
        return chosen

    wrap_x(xa, 0, WIN)
    for step in range(STEPS):
        z0 = step * SWEEPS
        nz = WIN - 2 * z0
        prepare(xa, step, z0, nz)
        sweep(xa, xb, None, betas[0], z0, nz, False)

        def pair(at, carry):
            sweep(xb, xa, pick(alphas, 1, at), pick(betas, 1, at), z0, nz, False)
            sweep(xa, xb, pick(alphas, 2, at), pick(betas, 2, at), z0, nz, False)
            return carry

        lax.fori_loop(0, (SWEEPS - 2) // 2, pair, 0)
        sweep(xb, xa, alphas[-1], betas[-1], z0 + SWEEPS, nz - 2 * SWEEPS, True)

    def put(kind, half, tile, block, value):
        out[pl.ds(((half * ZB + tile * 8) * 4 + kind) * 8 + block, 8, stride=32), :] = value

    for half in range(2):
        for tile in range(ZB // 8):
            ends = [xa[half * HALF + g + 1, pl.ds(PAD + HALO + tile * 8, 8), :] for g in range(8)]
            for g, value in enumerate(lane_groups(ends)):
                put(0, half, tile, block_of(g), value)
            sats = [sat[half * HALF + g, pl.ds(tile * 8, 8), :] for g in range(8)]
            for g, value in enumerate(lane_groups(sats)):
                put(1, half, tile, block_of(g), value)
            for block in range(BLOCKS):
                rows = block * ROWS + half * WIN + HALO + tile * 8
                put(2, half, tile, block, got[pl.ds(rows, 8), :])
                rows = block * ROWS + FIELDS * GROUP + half * ZB + tile * 8
                put(3, half, tile, block, got[pl.ds(rows, 8), :])

    place = (slot // ZB) * WIN + HALO + slot % ZB
    static[pl.ds(0, 8), :] = got[pl.ds(2 * GROUP + place, 8, stride=ROWS), :]
    static[pl.ds(8, 8), :] = got[pl.ds(1 * GROUP + place, 8, stride=ROWS), :]


def chain_kernel(coef, got, static, out, jumps, resids, factors, quads):
    b0, b1, b2 = coef[0], coef[1], coef[2]
    cond = static[pl.ds(0, 8), :]
    iron = static[pl.ds(8, 8), :]
    is_iron = iron > 0.5
    dt = STEPS * DT_FINE

    def part(n, kind):
        return got[pl.ds(n * 32 + kind * 8, 8), :]

    jump = jnp.zeros((8, NZ), jnp.float32)
    for n in range(SLICES):
        growth = jnp.exp(b1 * part(n, 1))
        lumped = 6.0 * jnp.where(is_iron, b2 + b0 * growth, 1.0)
        inverse = 1.0 / (cond + dt * lumped)
        factor = cond * inverse
        end = part(n, 0) + factor * jump
        out[pl.ds(n * 24, 8, stride=3), :] = end
        jumps[n] = jump
        resids[n] = end - part(n, 3)
        factors[n] = factor
        quads[n] = inverse * inverse
        if n < SLICES - 1:
            jump = end - part(n + 1, 2)

    tail = jnp.zeros((8, NZ), jnp.float32)
    grad = jnp.zeros((8, NZ), jnp.float32)
    sums = [jnp.zeros((8, NZ), jnp.float32) for _ in range(3)]
    for n in reversed(range(SLICES)):
        saturation = part(n, 1)
        growth = jnp.exp(b1 * saturation)
        lumped = 6.0 * jnp.where(is_iron, b2 + b0 * growth, 1.0)
        slope = resids[n] + tail
        scaled = slope * jumps[n] * quads[n]
        grad = grad + scaled * (dt * lumped)
        hterm = (6.0 * scaled) * (-dt * cond) * iron
        grown = hterm * growth
        sums[0] = sums[0] + grown
        sums[1] = sums[1] + grown * (b0 * saturation)
        sums[2] = sums[2] + hterm
        tail = factors[n] * slope
    lane = lax.broadcasted_iota(jnp.int32, (8, NZ), 1)
    totals = [jnp.sum(value, keepdims=True) for value in sums]
    row = jnp.where(lane == 0, totals[0], jnp.where(lane == 1, totals[1], jnp.where(lane == 2, totals[2], 0.0)))
    for n in range(SLICES):
        out[pl.ds(n * 24 + 1, 8, stride=3), :] = grad
        out[pl.ds(n * 24 + 2, 8, stride=3), :] = row


def unpack_kernel(got, end, grad, coef_grad):
    for kind, dest in enumerate((end, grad)):
        for half in range(2):
            flat = jnp.concatenate(
                [got[pl.ds(half * ZB * 24 + j * 3 + kind, ZB, stride=24), :] for j in range(BLOCKS)], axis=0
            )
            dest[pl.ds(half * HALF, HALF)] = jnp.transpose(flat).reshape(HALF, AB, NZ)
    sums = jnp.sum(got[pl.ds(2, SLICES * BLOCKS, stride=3), :], axis=0, keepdims=True)
    lane = lax.broadcasted_iota(jnp.int32, (1, NZ), 1)
    count = SLICES * BLOCKS * RB * AB * NZ
    for c in range(3):
        coef_grad[c] = jnp.sum(jnp.where(lane == c, sums, 0.0)) * (1.0 / count)


def vmem():
    return pl.BlockSpec(memory_space=pltpu.VMEM)


def smem():
    return pl.BlockSpec(memory_space=pltpu.SMEM)


def call(kernel, outs, ins, scratch, out_specs=None):
    spaces = {"s": pltpu.SMEM, "v": pltpu.VMEM, "h": pltpu.HBM}
    specs = [pl.BlockSpec(memory_space=spaces[place]) for place in ins]
    return pl.pallas_call(
        kernel,
        out_shape=outs,
        in_specs=specs,
        out_specs=out_specs if out_specs is not None else jax.tree.map(lambda leaf: vmem(), outs),
        scratch_shapes=scratch,
        compiler_params=pltpu.CompilerParams(vmem_limit_bytes=WHOLE_VMEM if "h" in ins else VMEM),
    )


def shape(*dims):
    return jax.ShapeDtypeStruct(dims, jnp.float32)


def solve(bh_coef, whole):
    block = pltpu.VMEM((RB, WIN, NZ), jnp.float32)
    return call(
        fine_kernel,
        (shape(SLICES * 32, NZ), shape(16, NZ)),
        "sv",
        [
            pltpu.VMEM((RB + 2, WIN + 2 * PAD, NZ), jnp.float32),
            pltpu.VMEM((RB + 2, WIN + 2 * PAD, NZ), jnp.float32),
            pltpu.VMEM((RB + 2, WIN + 2 * PAD, NZ), jnp.float32),
            block,
            block,
            block,
            pltpu.VMEM((RB, ZB, NZ), jnp.float32),
        ]
        + [block] * 8,
    )(bh_coef, whole)


def local(start_states, target, conductivity, material, current, bh_coef):
    field = pltpu.VMEM((RB, AB, NZ), jnp.float32)
    packed = call(
        pack_kernel,
        shape(BLOCKS * ROWS, NZ),
        "hhhhh",
        [field, field, field, pltpu.VMEM((RB, AB, NZ), jnp.int32), field, pltpu.SemaphoreType.DMA((5,))],
    )(start_states[0], target[0], conductivity, material, current)
    whole = lax.all_to_all(packed, ("azi", "rad"), 0, 0, tiled=True)
    fine, static = solve(bh_coef, whole)
    slices = lax.all_to_all(fine, "tm", 0, 0, tiled=True)
    line = pltpu.VMEM((SLICES, 8, NZ), jnp.float32)
    chained = call(chain_kernel, shape(SLICES * 24, NZ), "svv", [line] * 4)(bh_coef, slices, static)
    results = lax.all_to_all(
        chained.reshape(SLICES * BLOCKS, 1, 3 * NZ), ("tm", "azi", "rad"), 0, 0, tiled=True
    ).reshape(SLICES * 24, NZ)
    end, grad, coef_grad = call(
        unpack_kernel,
        (shape(RB, AB, NZ), shape(RB, AB, NZ), shape(3)),
        "v",
        [],
        out_specs=(vmem(), vmem(), smem()),
    )(results)
    return (end[None], grad, coef_grad)


def solution(mesh):
    placed = (
        P("tm", "rad", "azi", None),
        P("tm", "rad", "azi", None),
        P("rad", "azi", None),
        P("rad", "azi", None),
        P("rad", "azi", None),
        P(),
    )
    return jax.shard_map(
        local,
        mesh=mesh,
        in_specs=placed,
        out_specs=(P("tm", "rad", "azi", None), P("rad", "azi", None), P()),
        check_vma=False,
    )
```

```python
import functools
import math

import jax
import jax.numpy as jnp
from jax import lax
from jax.experimental import pallas as pl
from jax.experimental.pallas import tpu as pltpu
from jax.sharding import PartitionSpec as P

STEPS = 2
SWEEPS = 8
DT_FINE = 0.25
LOWER_EDGE = 0.05
UPPER_EDGE = 1.95

BLOCKS = 8
RADS = 4
RB = 16
AB = 16
NZ = 128
ZB = NZ // BLOCKS
HALO = 2 * SWEEPS
WIN = ZB + 2 * HALO
SLICES = 32
GROUP = 2 * WIN
FIELDS = 4
ROWS = FIELDS * GROUP + 2 * ZB
PAD = 8
VMEM = 48 * 1024 * 1024
WHOLE_VMEM = 56 * 1024 * 1024


STRIDES = ((4, 64), (2, 32), (1, 8))
INNER = 8


def rows_of(half):
    for t in range(16):
        yield ((t >> 1) & 1) * 8 + half * 4 + ((t >> 3) & 1) * 2 + ((t >> 2) & 1), t & 1


def lane_groups(tiles):
    tiles = list(tiles)
    lane = lax.broadcasted_iota(jnp.int32, tiles[0].shape, 1)
    for bit, stride in STRIDES:
        low = (lane & stride) == 0
        for i in range(8):
            if i & bit:
                continue
            first, second = tiles[i], tiles[i + bit]
            if 2 * stride == NZ:
                moved = pltpu.roll(jnp.where(low, second, first), stride, 1)
                tiles[i], tiles[i + bit] = jnp.where(low, first, moved), jnp.where(low, moved, second)
            else:
                tiles[i] = jnp.where(low, first, pltpu.roll(second, stride, 1))
                tiles[i + bit] = jnp.where(low, pltpu.roll(first, NZ - stride, 1), second)
    return tiles


def block_of(group):
    return (group % 2) * RADS + group // 2


def pack_kernel(start_at, target_at, cond_at, material_at, current_at, out, start, target, cond, material, current, sems):
    pairs = ((start_at, start), (material_at, material), (cond_at, cond), (current_at, current), (target_at, target))
    copies = [pltpu.make_async_copy(src, dst, sems.at[k]) for k, (src, dst) in enumerate(pairs)]
    for copy in copies:
        copy.start()

    def turned(read, half):
        return jnp.transpose(jnp.concatenate([read(r, pl.ds(q, 8, stride=2)) for r, q in rows_of(half)], axis=0))

    def put(field, half, read):
        edge = jnp.zeros((HALO, NZ), jnp.float32)
        padded = jnp.concatenate([edge, turned(read, half), edge], axis=0)
        for j in range(BLOCKS):
            out[pl.ds(j * ROWS + field * GROUP + half * WIN, WIN), :] = padded[ZB * j : ZB * j + WIN]

    copies[0].wait()
    for half in range(2):
        put(0, half, lambda r, q: start[r, q, :])
    copies[1].wait()
    for half in range(2):
        put(1, half, lambda r, q: jnp.where(material[r, q, :] == 1, 1.0, 0.0))
    copies[2].wait()
    for half in range(2):
        put(2, half, lambda r, q: cond[r, q, :])
    copies[3].wait()
    for half in range(2):
        put(3, half, lambda r, q: jnp.where(material[r, q, :] == 2, current[r, q, :], 0.0))
    copies[4].wait()
    for half in range(2):
        flat = turned(lambda r, q: target[r, q, :], half)
        for j in range(BLOCKS):
            out[pl.ds(j * ROWS + FIELDS * GROUP + half * ZB, ZB), :] = flat[ZB * j : ZB * (j + 1)]


def fine_kernel(coef, got, out, static, xa, xb, rho, iron, cond, source, sat, step_d, base, a_rp, a_rm, a_ap, a_am, a_zp, a_zm):
    b0, b1, b2 = coef[0], coef[1], coef[2]
    me = lax.axis_index("azi") * RADS + lax.axis_index("rad")
    slot = lax.axis_index("tm")

    def edged(q, s):
        return q * (INNER + 2) + s + 1

    def to_x(q, s, row, value):
        xa[edged(q, s), pl.ds(PAD + row, 8), :] = value

    def to(ref):
        def put(q, s, row, value):
            ref[q * INNER + s, pl.ds(row, 8), :] = value

        return put

    def some(tile, carry):
        row = pl.multiple_of(tile * 8, 8)
        for field, dest in ((0, to_x), (1, to(iron)), (2, to(cond)), (3, to(source))):
            for half in range(2):
                rows = field * GROUP + half * WIN + row
                tiles = [got[pl.ds(pl.multiple_of(block_of(g) * ROWS + rows, 8), 8), :] for g in range(8)]
                for g, value in enumerate(lane_groups(tiles)):
                    dest(g & 1, half * 4 + (g >> 1), row, value)
        return carry

    lax.fori_loop(0, WIN // 8, some, 0)

    blank = jnp.zeros((PAD, NZ), jnp.float32)
    for i in range(2 * (INNER + 2)):
        for x in (xa, xb):
            x[i, pl.ds(0, PAD), :] = blank
            x[i, pl.ds(PAD + WIN, PAD), :] = blank
        rho[i, pl.ds(0, PAD), :] = blank + 1.0
        rho[i, pl.ds(PAD + WIN, PAD), :] = blank + 1.0

    def wrap(get, put, size, outside):
        lane = lax.broadcasted_iota(jnp.int32, (size, NZ), 1)
        for q in range(2):
            last = pltpu.roll(get(edged(q, INNER - 1)), 16, 1)
            put(edged(q, -1), jnp.where(lane < 16, outside, last))
            first = pltpu.roll(get(edged(q, 0)), NZ - 16, 1)
            put(edged(q, INNER), jnp.where(lane >= NZ - 16, outside, first))

    def wrap_x(x, z0, nz):
        rows = pl.ds(PAD + z0, nz)

        def put(i, value):
            x[i, rows, :] = value

        wrap(lambda i: x[i, rows, :], put, nz, 0.0)

    def wrap_rho(z0, nz):
        rows = pl.ds(PAD + z0, nz)

        def put(i, value):
            rho[i, rows, :] = value

        wrap(lambda i: rho[i, rows, :], put, nz, 1.0)

    def prepare(x, step, z0, nz):
        lane = lax.broadcasted_iota(jnp.int32, (nz, NZ), 1) & 15
        row = lax.broadcasted_iota(jnp.int32, (nz, NZ), 0) + (z0 - HALO) + me * ZB
        rows = pl.ds(PAD + z0, nz)
        own = pl.ds(z0, nz)

        def azimuths(ref, q, s, outside):
            beside = ref[edged(1 - q, s), rows, :]
            if q == 0:
                return beside, jnp.where(lane == 0, outside, pltpu.roll(beside, 1, 1))
            return jnp.where(lane == 15, outside, pltpu.roll(beside, NZ - 1, 1)), beside

        for q in range(2):
            for s in range(INNER):
                i, at = q * INNER + s, edged(q, s)
                radial = 0.5 * (x[at + 1, rows, :] - x[at - 1, rows, :])
                up, down = azimuths(x, q, s, 0.0)
                azimuthal = 0.5 * (up - down)
                square = radial * radial + azimuthal * azimuthal
                saturation = square / (1.0 + square)
                value = b2 + b0 * jnp.exp(b1 * saturation)
                rho[at, rows, :] = jnp.where(iron[i, own, :] > 0.5, value, 1.0)
                if step == 0:
                    sat[i] = saturation[HALO - z0 : HALO - z0 + ZB]

        wrap_rho(z0, nz)
        angle = (4.0 * math.pi / (SLICES * STEPS)) * (slot * STEPS + (step + 1)).astype(jnp.float32)
        wave = jnp.cos(jnp.full((8, NZ), angle, jnp.float32))[0:1]

        for q in range(2):
            for s in range(INNER):
                i, at = q * INNER + s, edged(q, s)
                centre = rho[at, rows, :]
                up, down = azimuths(rho, q, s, 1.0)
                rp = 0.5 * (centre + rho[at + 1, rows, :])
                rm = 0.5 * (centre + rho[at - 1, rows, :])
                ap = 0.5 * (centre + up)
                am = 0.5 * (centre + down)
                zp = 0.5 * (centre + rho[at, pl.ds(PAD + z0 + 1, nz), :])
                zm = 0.5 * (centre + rho[at, pl.ds(PAD + z0 - 1, nz), :])
                mass = cond[i, own, :] * (1.0 / DT_FINE)
                inverse = 1.0 / (mass + rp + rm + ap + am + zp + zm)
                a_rp[i, own, :] = inverse * rp
                a_rm[i, own, :] = inverse * rm
                a_ap[i, own, :] = jnp.where(lane == 15, 0.0, inverse * ap) if q else inverse * ap
                a_am[i, own, :] = inverse * am if q else jnp.where(lane == 0, 0.0, inverse * am)
                a_zp[i, own, :] = jnp.where(row == NZ - 1, 0.0, inverse * zp)
                a_zm[i, own, :] = jnp.where(row == 0, 0.0, inverse * zm)
                base[i, own, :] = inverse * (mass * x[at, rows, :] + wave * source[i, own, :])

    def sweep(x, fresh, alpha, beta, z0, nz, final):
        rows = pl.ds(PAD + z0, nz)
        own = pl.ds(z0, nz)
        lane = lax.broadcasted_iota(jnp.int32, (nz, NZ), 1)
        for s in range(INNER):
            for q in range(2):
                i, at = q * INNER + s, edged(q, s)
                centre = x[at, rows, :]
                beside = x[edged(1 - q, s), rows, :]
                rolled = pltpu.roll(beside, NZ - 1 if q else 1, 1)
                up, down = (rolled, beside) if q else (beside, rolled)
                total = base[i, own, :] - centre
                total = total + a_rp[i, own, :] * x[at + 1, rows, :]
                total = total + a_rm[i, own, :] * x[at - 1, rows, :]
                total = total + a_ap[i, own, :] * up
                total = total + a_am[i, own, :] * down
                total = total + a_zp[i, own, :] * x[at, pl.ds(PAD + z0 + 1, nz), :]
                total = total + a_zm[i, own, :] * x[at, pl.ds(PAD + z0 - 1, nz), :]
                change = beta * total
                if alpha is not None:
                    change = change + alpha * step_d[i, own, :]
                if not final:
                    step_d[i, own, :] = change
                value = centre + change
                fresh[at, rows, :] = value
                if s == 0:
                    first = pltpu.roll(value, NZ - 16, 1)
                    fresh[edged(q, INNER), rows, :] = jnp.where(lane >= NZ - 16, 0.0, first)
                if s == INNER - 1:
                    last = pltpu.roll(value, 16, 1)
                    fresh[edged(q, -1), rows, :] = jnp.where(lane < 16, 0.0, last)

    theta = 0.5 * (UPPER_EDGE + LOWER_EDGE)
    delta = 0.5 * (UPPER_EDGE - LOWER_EDGE)
    scaled = theta / delta
    ratio, alphas, betas = 1.0 / scaled, [0.0], [1.0 / theta]
    for index in range(SWEEPS - 1):
        following = 1.0 / (2.0 * scaled - ratio)
        alphas.append(following * ratio)
        betas.append(2.0 * following / delta)
        ratio = following

    def pick(values, first, at):
        chosen = jnp.float32(values[first])
        for k in range(1, (SWEEPS - first) // 2):
            chosen = jnp.where(at == k, jnp.float32(values[first + 2 * k]), chosen)
        return chosen

    wrap_x(xa, 0, WIN)
    for step in range(STEPS):
        z0 = step * SWEEPS
        nz = WIN - 2 * z0
        prepare(xa, step, z0, nz)
        sweep(xa, xb, None, betas[0], z0, nz, False)

        def pair(at, carry):
            sweep(xb, xa, pick(alphas, 1, at), pick(betas, 1, at), z0, nz, False)
            sweep(xa, xb, pick(alphas, 2, at), pick(betas, 2, at), z0, nz, False)
            return carry

        lax.fori_loop(0, (SWEEPS - 2) // 2, pair, 0)
        sweep(xb, xa, alphas[-1], betas[-1], z0 + SWEEPS, nz - 2 * SWEEPS, True)

    def put(kind, half, tile, block, value):
        out[pl.ds(((half * ZB + tile * 8) * 4 + kind) * 8 + block, 8, stride=32), :] = value

    for half in range(2):
        for tile in range(ZB // 8):
            ends = [xa[edged(g & 1, half * 4 + (g >> 1)), pl.ds(PAD + HALO + tile * 8, 8), :] for g in range(8)]
            for g, value in enumerate(lane_groups(ends)):
                put(0, half, tile, block_of(g), value)
            sats = [sat[(g & 1) * INNER + half * 4 + (g >> 1), pl.ds(tile * 8, 8), :] for g in range(8)]
            for g, value in enumerate(lane_groups(sats)):
                put(1, half, tile, block_of(g), value)
            for block in range(BLOCKS):
                rows = block * ROWS + half * WIN + HALO + tile * 8
                put(2, half, tile, block, got[pl.ds(rows, 8), :])
                rows = block * ROWS + FIELDS * GROUP + half * ZB + tile * 8
                put(3, half, tile, block, got[pl.ds(rows, 8), :])

    place = (slot // ZB) * WIN + HALO + slot % ZB
    static[pl.ds(0, 8), :] = got[pl.ds(2 * GROUP + place, 8, stride=ROWS), :]
    static[pl.ds(8, 8), :] = got[pl.ds(1 * GROUP + place, 8, stride=ROWS), :]


def chain_kernel(coef, got, static, out, jumps, resids, factors, quads):
    b0, b1, b2 = coef[0], coef[1], coef[2]
    cond = static[pl.ds(0, 8), :]
    iron = static[pl.ds(8, 8), :]
    is_iron = iron > 0.5
    dt = STEPS * DT_FINE

    def part(n, kind):
        return got[pl.ds(n * 32 + kind * 8, 8), :]

    jump = jnp.zeros((8, NZ), jnp.float32)
    for n in range(SLICES):
        growth = jnp.exp(b1 * part(n, 1))
        lumped = 6.0 * jnp.where(is_iron, b2 + b0 * growth, 1.0)
        inverse = 1.0 / (cond + dt * lumped)
        factor = cond * inverse
        end = part(n, 0) + factor * jump
        out[pl.ds(n * 24, 8, stride=3), :] = end
        jumps[n] = jump
        resids[n] = end - part(n, 3)
        factors[n] = factor
        quads[n] = inverse * inverse
        if n < SLICES - 1:
            jump = end - part(n + 1, 2)

    tail = jnp.zeros((8, NZ), jnp.float32)
    grad = jnp.zeros((8, NZ), jnp.float32)
    sums = [jnp.zeros((8, NZ), jnp.float32) for _ in range(3)]
    for n in reversed(range(SLICES)):
        saturation = part(n, 1)
        growth = jnp.exp(b1 * saturation)
        lumped = 6.0 * jnp.where(is_iron, b2 + b0 * growth, 1.0)
        slope = resids[n] + tail
        scaled = slope * jumps[n] * quads[n]
        grad = grad + scaled * (dt * lumped)
        hterm = (6.0 * scaled) * (-dt * cond) * iron
        grown = hterm * growth
        sums[0] = sums[0] + grown
        sums[1] = sums[1] + grown * (b0 * saturation)
        sums[2] = sums[2] + hterm
        tail = factors[n] * slope
    lane = lax.broadcasted_iota(jnp.int32, (8, NZ), 1)
    totals = [jnp.sum(value, keepdims=True) for value in sums]
    row = jnp.where(lane == 0, totals[0], jnp.where(lane == 1, totals[1], jnp.where(lane == 2, totals[2], 0.0)))
    for n in range(SLICES):
        out[pl.ds(n * 24 + 1, 8, stride=3), :] = grad
        out[pl.ds(n * 24 + 2, 8, stride=3), :] = row


def unpack_kernel(got, end, grad, coef_grad):
    for kind, dest in enumerate((end, grad)):
        for half in range(2):
            flat = jnp.concatenate(
                [got[pl.ds(half * ZB * 24 + j * 3 + kind, ZB, stride=24), :] for j in range(BLOCKS)], axis=0
            )
            turned = jnp.transpose(flat)
            for t, (r, q) in enumerate(rows_of(half)):
                dest[r, pl.ds(q, 8, stride=2), :] = turned[8 * t : 8 * t + 8]
    sums = jnp.sum(got[pl.ds(2, SLICES * BLOCKS, stride=3), :], axis=0, keepdims=True)
    lane = lax.broadcasted_iota(jnp.int32, (1, NZ), 1)
    count = SLICES * BLOCKS * RB * AB * NZ
    for c in range(3):
        coef_grad[c] = jnp.sum(jnp.where(lane == c, sums, 0.0)) * (1.0 / count)


def vmem():
    return pl.BlockSpec(memory_space=pltpu.VMEM)


def smem():
    return pl.BlockSpec(memory_space=pltpu.SMEM)


def call(kernel, outs, ins, scratch, out_specs=None):
    spaces = {"s": pltpu.SMEM, "v": pltpu.VMEM, "h": pltpu.HBM}
    specs = [pl.BlockSpec(memory_space=spaces[place]) for place in ins]
    return pl.pallas_call(
        kernel,
        out_shape=outs,
        in_specs=specs,
        out_specs=out_specs if out_specs is not None else jax.tree.map(lambda leaf: vmem(), outs),
        scratch_shapes=scratch,
        compiler_params=pltpu.CompilerParams(vmem_limit_bytes=WHOLE_VMEM if "h" in ins else VMEM),
    )


def shape(*dims):
    return jax.ShapeDtypeStruct(dims, jnp.float32)


def solve(bh_coef, whole):
    block = pltpu.VMEM((RB, WIN, NZ), jnp.float32)
    return call(
        fine_kernel,
        (shape(SLICES * 32, NZ), shape(16, NZ)),
        "sv",
        [
            pltpu.VMEM((2 * (INNER + 2), WIN + 2 * PAD, NZ), jnp.float32),
            pltpu.VMEM((2 * (INNER + 2), WIN + 2 * PAD, NZ), jnp.float32),
            pltpu.VMEM((2 * (INNER + 2), WIN + 2 * PAD, NZ), jnp.float32),
            block,
            block,
            block,
            pltpu.VMEM((RB, ZB, NZ), jnp.float32),
        ]
        + [block] * 8,
    )(bh_coef, whole)


def local(start_states, target, conductivity, material, current, bh_coef):
    field = pltpu.VMEM((RB, AB, NZ), jnp.float32)
    packed = call(
        pack_kernel,
        shape(BLOCKS * ROWS, NZ),
        "hhhhh",
        [field, field, field, pltpu.VMEM((RB, AB, NZ), jnp.int32), field, pltpu.SemaphoreType.DMA((5,))],
    )(start_states[0], target[0], conductivity, material, current)
    whole = lax.all_to_all(packed, ("azi", "rad"), 0, 0, tiled=True)
    fine, static = solve(bh_coef, whole)
    slices = lax.all_to_all(fine, "tm", 0, 0, tiled=True)
    line = pltpu.VMEM((SLICES, 8, NZ), jnp.float32)
    chained = call(chain_kernel, shape(SLICES * 24, NZ), "svv", [line] * 4)(bh_coef, slices, static)
    results = lax.all_to_all(
        chained.reshape(SLICES * BLOCKS, 1, 3 * NZ), ("tm", "azi", "rad"), 0, 0, tiled=True
    ).reshape(SLICES * 24, NZ)
    end, grad, coef_grad = call(
        unpack_kernel,
        (shape(RB, AB, NZ), shape(RB, AB, NZ), shape(3)),
        "v",
        [],
        out_specs=(vmem(), vmem(), smem()),
    )(results)
    return (end[None], grad, coef_grad)


def solution(mesh):
    placed = (
        P("tm", "rad", "azi", None),
        P("tm", "rad", "azi", None),
        P("rad", "azi", None),
        P("rad", "azi", None),
        P("rad", "azi", None),
        P(),
    )
    return jax.shard_map(
        local,
        mesh=mesh,
        in_specs=placed,
        out_specs=(P("tm", "rad", "azi", None), P("rad", "azi", None), P()),
        check_vma=False,
    )
```

```python
import functools
import math

import jax
import jax.numpy as jnp
from jax import lax
from jax.experimental import pallas as pl
from jax.experimental.pallas import tpu as pltpu
from jax.sharding import PartitionSpec as P

STEPS = 2
SWEEPS = 8
DT_FINE = 0.25
LOWER_EDGE = 0.05
UPPER_EDGE = 1.95

BLOCKS = 8
RADS = 4
RB = 16
AB = 16
NZ = 128
ZB = NZ // BLOCKS
HALO = 2 * SWEEPS
WIN = ZB + 2 * HALO
SLICES = 32
GROUP = 2 * WIN
FIELDS = 4
ROWS = FIELDS * GROUP + 2 * ZB
PAD = 8
VMEM = 48 * 1024 * 1024
WHOLE_VMEM = 56 * 1024 * 1024


STRIDES = ((4, 64), (2, 32), (1, 8))
INNER = 8


def rows_of(half):
    for t in range(16):
        yield ((t >> 1) & 1) * 8 + half * 4 + ((t >> 3) & 1) * 2 + ((t >> 2) & 1), t & 1


def lane_groups(tiles):
    tiles = list(tiles)
    lane = lax.broadcasted_iota(jnp.int32, tiles[0].shape, 1)
    for bit, stride in STRIDES:
        low = (lane & stride) == 0
        for i in range(8):
            if i & bit:
                continue
            first, second = tiles[i], tiles[i + bit]
            if 2 * stride == NZ:
                moved = pltpu.roll(jnp.where(low, second, first), stride, 1)
                tiles[i], tiles[i + bit] = jnp.where(low, first, moved), jnp.where(low, moved, second)
            else:
                tiles[i] = jnp.where(low, first, pltpu.roll(second, stride, 1))
                tiles[i + bit] = jnp.where(low, pltpu.roll(first, NZ - stride, 1), second)
    return tiles


def block_of(group):
    return (group % 2) * RADS + group // 2


def pack_kernel(start_at, target_at, cond_at, material_at, current_at, out_at, start, target, cond, material, current, out, sems, sent):
    pairs = ((start_at, start), (material_at, material), (cond_at, cond), (current_at, current), (target_at, target))
    copies = [pltpu.make_async_copy(src, dst, sems.at[k]) for k, (src, dst) in enumerate(pairs)]
    for copy in copies:
        copy.start()

    def turned(read, half):
        return jnp.transpose(jnp.concatenate([read(r, pl.ds(q, 8, stride=2)) for r, q in rows_of(half)], axis=0))

    def put(field, half, read):
        edge = jnp.zeros((HALO, NZ), jnp.float32)
        padded = jnp.concatenate([edge, turned(read, half), edge], axis=0)
        for j in range(BLOCKS):
            out[j, pl.ds(field * GROUP + half * WIN, WIN), :] = padded[ZB * j : ZB * j + WIN]

    sends = []

    def send(field, size):
        rows = pl.ds(field * GROUP, size)
        sends.append(pltpu.make_async_copy(out.at[:, rows, :], out_at.at[:, rows, :], sent.at[field]))
        sends[-1].start()

    copies[0].wait()
    for half in range(2):
        put(0, half, lambda r, q: start[r, q, :])
    send(0, GROUP)
    copies[1].wait()
    for half in range(2):
        put(1, half, lambda r, q: jnp.where(material[r, q, :] == 1, 1.0, 0.0))
    send(1, GROUP)
    copies[2].wait()
    for half in range(2):
        put(2, half, lambda r, q: cond[r, q, :])
    send(2, GROUP)
    copies[3].wait()
    for half in range(2):
        put(3, half, lambda r, q: jnp.where(material[r, q, :] == 2, current[r, q, :], 0.0))
    send(3, GROUP)
    copies[4].wait()
    for half in range(2):
        flat = turned(lambda r, q: target[r, q, :], half)
        for j in range(BLOCKS):
            out[j, pl.ds(FIELDS * GROUP + half * ZB, ZB), :] = flat[ZB * j : ZB * (j + 1)]
    send(4, 2 * ZB)
    for copy in sends:
        copy.wait()


def fine_kernel(coef, got, out, static, xa, xb, rho, iron, cond, source, sat, step_d, base, a_rp, a_rm, a_ap, a_am, a_zp, a_zm):
    b0, b1, b2 = coef[0], coef[1], coef[2]
    me = lax.axis_index("azi") * RADS + lax.axis_index("rad")
    slot = lax.axis_index("tm")

    def edged(q, s):
        return q * (INNER + 2) + s + 1

    def to_x(q, s, row, value):
        xa[edged(q, s), pl.ds(PAD + row, 8), :] = value

    def to(ref):
        def put(q, s, row, value):
            ref[q * INNER + s, pl.ds(row, 8), :] = value

        return put

    def some(tile, carry):
        row = pl.multiple_of(tile * 8, 8)
        for field, dest in ((0, to_x), (1, to(iron)), (2, to(cond)), (3, to(source))):
            for half in range(2):
                rows = field * GROUP + half * WIN + row
                tiles = [got[pl.ds(pl.multiple_of(block_of(g) * ROWS + rows, 8), 8), :] for g in range(8)]
                for g, value in enumerate(lane_groups(tiles)):
                    dest(g & 1, half * 4 + (g >> 1), row, value)
        return carry

    lax.fori_loop(0, WIN // 8, some, 0)

    blank = jnp.zeros((PAD, NZ), jnp.float32)
    for i in range(2 * (INNER + 2)):
        for x in (xa, xb):
            x[i, pl.ds(0, PAD), :] = blank
            x[i, pl.ds(PAD + WIN, PAD), :] = blank
        rho[i, pl.ds(0, PAD), :] = blank + 1.0
        rho[i, pl.ds(PAD + WIN, PAD), :] = blank + 1.0

    def wrap(get, put, size, outside):
        lane = lax.broadcasted_iota(jnp.int32, (size, NZ), 1)
        for q in range(2):
            last = pltpu.roll(get(edged(q, INNER - 1)), 16, 1)
            put(edged(q, -1), jnp.where(lane < 16, outside, last))
            first = pltpu.roll(get(edged(q, 0)), NZ - 16, 1)
            put(edged(q, INNER), jnp.where(lane >= NZ - 16, outside, first))

    def wrap_x(x, z0, nz):
        rows = pl.ds(PAD + z0, nz)

        def put(i, value):
            x[i, rows, :] = value

        wrap(lambda i: x[i, rows, :], put, nz, 0.0)

    def wrap_rho(z0, nz):
        rows = pl.ds(PAD + z0, nz)

        def put(i, value):
            rho[i, rows, :] = value

        wrap(lambda i: rho[i, rows, :], put, nz, 1.0)

    def prepare(x, step, z0, nz):
        lane = lax.broadcasted_iota(jnp.int32, (nz, NZ), 1) & 15
        row = lax.broadcasted_iota(jnp.int32, (nz, NZ), 0) + (z0 - HALO) + me * ZB
        rows = pl.ds(PAD + z0, nz)
        own = pl.ds(z0, nz)

        def azimuths(ref, q, s, outside):
            beside = ref[edged(1 - q, s), rows, :]
            if q == 0:
                return beside, jnp.where(lane == 0, outside, pltpu.roll(beside, 1, 1))
            return jnp.where(lane == 15, outside, pltpu.roll(beside, NZ - 1, 1)), beside

        for q in range(2):
            for s in range(INNER):
                i, at = q * INNER + s, edged(q, s)
                radial = 0.5 * (x[at + 1, rows, :] - x[at - 1, rows, :])
                up, down = azimuths(x, q, s, 0.0)
                azimuthal = 0.5 * (up - down)
                square = radial * radial + azimuthal * azimuthal
                saturation = square / (1.0 + square)
                value = b2 + b0 * jnp.exp(b1 * saturation)
                rho[at, rows, :] = jnp.where(iron[i, own, :] > 0.5, value, 1.0)
                if step == 0:
                    sat[i] = saturation[HALO - z0 : HALO - z0 + ZB]

        wrap_rho(z0, nz)
        angle = (4.0 * math.pi / (SLICES * STEPS)) * (slot * STEPS + (step + 1)).astype(jnp.float32)
        wave = jnp.cos(jnp.full((8, NZ), angle, jnp.float32))[0:1]

        for q in range(2):
            for s in range(INNER):
                i, at = q * INNER + s, edged(q, s)
                centre = rho[at, rows, :]
                up, down = azimuths(rho, q, s, 1.0)
                rp = 0.5 * (centre + rho[at + 1, rows, :])
                rm = 0.5 * (centre + rho[at - 1, rows, :])
                ap = 0.5 * (centre + up)
                am = 0.5 * (centre + down)
                zp = 0.5 * (centre + rho[at, pl.ds(PAD + z0 + 1, nz), :])
                zm = 0.5 * (centre + rho[at, pl.ds(PAD + z0 - 1, nz), :])
                mass = cond[i, own, :] * (1.0 / DT_FINE)
                inverse = 1.0 / (mass + rp + rm + ap + am + zp + zm)
                a_rp[i, own, :] = inverse * rp
                a_rm[i, own, :] = inverse * rm
                a_ap[i, own, :] = jnp.where(lane == 15, 0.0, inverse * ap) if q else inverse * ap
                a_am[i, own, :] = inverse * am if q else jnp.where(lane == 0, 0.0, inverse * am)
                a_zp[i, own, :] = jnp.where(row == NZ - 1, 0.0, inverse * zp)
                a_zm[i, own, :] = jnp.where(row == 0, 0.0, inverse * zm)
                base[i, own, :] = inverse * (mass * x[at, rows, :] + wave * source[i, own, :])

    def sweep(x, fresh, alpha, beta, z0, nz, final):
        rows = pl.ds(PAD + z0, nz)
        own = pl.ds(z0, nz)
        lane = lax.broadcasted_iota(jnp.int32, (nz, NZ), 1)
        below = [x[edged(q, -1), rows, :] for q in range(2)]
        middle = [x[edged(q, 0), rows, :] for q in range(2)]
        for s in range(INNER):
            above = [x[edged(q, s + 1), rows, :] for q in range(2)]
            for q in range(2):
                i, at = q * INNER + s, edged(q, s)
                centre, beside = middle[q], middle[1 - q]
                rolled = pltpu.roll(beside, NZ - 1 if q else 1, 1)
                up, down = (rolled, beside) if q else (beside, rolled)
                total = base[i, own, :] - centre
                total = total + a_rp[i, own, :] * above[q]
                total = total + a_rm[i, own, :] * below[q]
                total = total + a_zp[i, own, :] * x[at, pl.ds(PAD + z0 + 1, nz), :]
                total = total + a_zm[i, own, :] * x[at, pl.ds(PAD + z0 - 1, nz), :]
                total = total + (a_ap[i, own, :] * up + a_am[i, own, :] * down)
                change = beta * total
                if alpha is not None:
                    change = change + alpha * step_d[i, own, :]
                if not final:
                    step_d[i, own, :] = change
                value = centre + change
                fresh[at, rows, :] = value
                if s == 0:
                    first = pltpu.roll(value, NZ - 16, 1)
                    fresh[edged(q, INNER), rows, :] = jnp.where(lane >= NZ - 16, 0.0, first)
                if s == INNER - 1:
                    last = pltpu.roll(value, 16, 1)
                    fresh[edged(q, -1), rows, :] = jnp.where(lane < 16, 0.0, last)
            below, middle = middle, above

    theta = 0.5 * (UPPER_EDGE + LOWER_EDGE)
    delta = 0.5 * (UPPER_EDGE - LOWER_EDGE)
    scaled = theta / delta
    ratio, alphas, betas = 1.0 / scaled, [0.0], [1.0 / theta]
    for index in range(SWEEPS - 1):
        following = 1.0 / (2.0 * scaled - ratio)
        alphas.append(following * ratio)
        betas.append(2.0 * following / delta)
        ratio = following

    def pick(values, first, at):
        chosen = jnp.float32(values[first])
        for k in range(1, (SWEEPS - first) // 2):
            chosen = jnp.where(at == k, jnp.float32(values[first + 2 * k]), chosen)
        return chosen

    wrap_x(xa, 0, WIN)
    for step in range(STEPS):
        z0 = step * SWEEPS
        nz = WIN - 2 * z0
        prepare(xa, step, z0, nz)
        sweep(xa, xb, None, betas[0], z0, nz, False)

        def pair(at, carry):
            sweep(xb, xa, pick(alphas, 1, at), pick(betas, 1, at), z0, nz, False)
            sweep(xa, xb, pick(alphas, 2, at), pick(betas, 2, at), z0, nz, False)
            return carry

        lax.fori_loop(0, (SWEEPS - 2) // 2, pair, 0)
        sweep(xb, xa, alphas[-1], betas[-1], z0 + SWEEPS, nz - 2 * SWEEPS, True)

    def put(kind, half, tile, block, value):
        out[pl.ds(((half * ZB + tile * 8) * 4 + kind) * 8 + block, 8, stride=32), :] = value

    for half in range(2):
        for tile in range(ZB // 8):
            ends = [xa[edged(g & 1, half * 4 + (g >> 1)), pl.ds(PAD + HALO + tile * 8, 8), :] for g in range(8)]
            for g, value in enumerate(lane_groups(ends)):
                put(0, half, tile, block_of(g), value)
            sats = [sat[(g & 1) * INNER + half * 4 + (g >> 1), pl.ds(tile * 8, 8), :] for g in range(8)]
            for g, value in enumerate(lane_groups(sats)):
                put(1, half, tile, block_of(g), value)
            for block in range(BLOCKS):
                rows = block * ROWS + half * WIN + HALO + tile * 8
                put(2, half, tile, block, got[pl.ds(rows, 8), :])
                rows = block * ROWS + FIELDS * GROUP + half * ZB + tile * 8
                put(3, half, tile, block, got[pl.ds(rows, 8), :])

    place = (slot // ZB) * WIN + HALO + slot % ZB
    static[pl.ds(0, 8), :] = got[pl.ds(2 * GROUP + place, 8, stride=ROWS), :]
    static[pl.ds(8, 8), :] = got[pl.ds(1 * GROUP + place, 8, stride=ROWS), :]


def chain_kernel(coef, got, static, out, jumps, resids, factors, quads):
    b0, b1, b2 = coef[0], coef[1], coef[2]
    cond = static[pl.ds(0, 8), :]
    iron = static[pl.ds(8, 8), :]
    is_iron = iron > 0.5
    dt = STEPS * DT_FINE

    def part(n, kind):
        return got[pl.ds(n * 32 + kind * 8, 8), :]

    jump = jnp.zeros((8, NZ), jnp.float32)
    for n in range(SLICES):
        growth = jnp.exp(b1 * part(n, 1))
        lumped = 6.0 * jnp.where(is_iron, b2 + b0 * growth, 1.0)
        inverse = 1.0 / (cond + dt * lumped)
        factor = cond * inverse
        end = part(n, 0) + factor * jump
        out[pl.ds(n * 24, 8, stride=3), :] = end
        jumps[n] = jump
        resids[n] = end - part(n, 3)
        factors[n] = factor
        quads[n] = inverse * inverse
        if n < SLICES - 1:
            jump = end - part(n + 1, 2)

    tail = jnp.zeros((8, NZ), jnp.float32)
    grad = jnp.zeros((8, NZ), jnp.float32)
    sums = [jnp.zeros((8, NZ), jnp.float32) for _ in range(3)]
    for n in reversed(range(SLICES)):
        saturation = part(n, 1)
        growth = jnp.exp(b1 * saturation)
        lumped = 6.0 * jnp.where(is_iron, b2 + b0 * growth, 1.0)
        slope = resids[n] + tail
        scaled = slope * jumps[n] * quads[n]
        grad = grad + scaled * (dt * lumped)
        hterm = (6.0 * scaled) * (-dt * cond) * iron
        grown = hterm * growth
        sums[0] = sums[0] + grown
        sums[1] = sums[1] + grown * (b0 * saturation)
        sums[2] = sums[2] + hterm
        tail = factors[n] * slope
    lane = lax.broadcasted_iota(jnp.int32, (8, NZ), 1)
    totals = [jnp.sum(value, keepdims=True) for value in sums]
    row = jnp.where(lane == 0, totals[0], jnp.where(lane == 1, totals[1], jnp.where(lane == 2, totals[2], 0.0)))
    for n in range(SLICES):
        out[pl.ds(n * 24 + 1, 8, stride=3), :] = grad
        out[pl.ds(n * 24 + 2, 8, stride=3), :] = row


def unpack_kernel(got, end, grad, coef_grad):
    for kind, dest in enumerate((end, grad)):
        for half in range(2):
            flat = jnp.concatenate(
                [got[pl.ds(half * ZB * 24 + j * 3 + kind, ZB, stride=24), :] for j in range(BLOCKS)], axis=0
            )
            turned = jnp.transpose(flat)
            for t, (r, q) in enumerate(rows_of(half)):
                dest[r, pl.ds(q, 8, stride=2), :] = turned[8 * t : 8 * t + 8]
    sums = jnp.sum(got[pl.ds(2, SLICES * BLOCKS, stride=3), :], axis=0, keepdims=True)
    lane = lax.broadcasted_iota(jnp.int32, (1, NZ), 1)
    count = SLICES * BLOCKS * RB * AB * NZ
    for c in range(3):
        coef_grad[c] = jnp.sum(jnp.where(lane == c, sums, 0.0)) * (1.0 / count)


def vmem():
    return pl.BlockSpec(memory_space=pltpu.VMEM)


def smem():
    return pl.BlockSpec(memory_space=pltpu.SMEM)


def call(kernel, outs, ins, scratch, out_specs=None):
    spaces = {"s": pltpu.SMEM, "v": pltpu.VMEM, "h": pltpu.HBM}
    specs = [pl.BlockSpec(memory_space=spaces[place]) for place in ins]
    return pl.pallas_call(
        kernel,
        out_shape=outs,
        in_specs=specs,
        out_specs=out_specs if out_specs is not None else jax.tree.map(lambda leaf: vmem(), outs),
        scratch_shapes=scratch,
        compiler_params=pltpu.CompilerParams(vmem_limit_bytes=WHOLE_VMEM if "h" in ins else VMEM),
    )


def shape(*dims):
    return jax.ShapeDtypeStruct(dims, jnp.float32)


def solve(bh_coef, whole):
    block = pltpu.VMEM((RB, WIN, NZ), jnp.float32)
    return call(
        fine_kernel,
        (shape(SLICES * 32, NZ), shape(16, NZ)),
        "sv",
        [
            pltpu.VMEM((2 * (INNER + 2), WIN + 2 * PAD, NZ), jnp.float32),
            pltpu.VMEM((2 * (INNER + 2), WIN + 2 * PAD, NZ), jnp.float32),
            pltpu.VMEM((2 * (INNER + 2), WIN + 2 * PAD, NZ), jnp.float32),
            block,
            block,
            block,
            pltpu.VMEM((RB, ZB, NZ), jnp.float32),
        ]
        + [block] * 8,
    )(bh_coef, whole)


def local(start_states, target, conductivity, material, current, bh_coef):
    field = pltpu.VMEM((RB, AB, NZ), jnp.float32)
    packed = call(
        pack_kernel,
        shape(BLOCKS, ROWS, NZ),
        "hhhhh",
        [field, field, field, pltpu.VMEM((RB, AB, NZ), jnp.int32), field, pltpu.VMEM((BLOCKS, ROWS, NZ), jnp.float32)]
        + [pltpu.SemaphoreType.DMA((5,))] * 2,
        out_specs=pl.BlockSpec(memory_space=pltpu.HBM),
    )(start_states[0], target[0], conductivity, material, current).reshape(BLOCKS * ROWS, NZ)
    whole = lax.all_to_all(packed, ("azi", "rad"), 0, 0, tiled=True)
    fine, static = solve(bh_coef, whole)
    slices = lax.all_to_all(fine, "tm", 0, 0, tiled=True)
    line = pltpu.VMEM((SLICES, 8, NZ), jnp.float32)
    chained = call(chain_kernel, shape(SLICES * 24, NZ), "svv", [line] * 4)(bh_coef, slices, static)
    results = lax.all_to_all(
        chained.reshape(SLICES * BLOCKS, 1, 3 * NZ), ("tm", "azi", "rad"), 0, 0, tiled=True
    ).reshape(SLICES * 24, NZ)
    end, grad, coef_grad = call(
        unpack_kernel,
        (shape(RB, AB, NZ), shape(RB, AB, NZ), shape(3)),
        "v",
        [],
        out_specs=(vmem(), vmem(), smem()),
    )(results)
    return (end[None], grad, coef_grad)


def solution(mesh):
    placed = (
        P("tm", "rad", "azi", None),
        P("tm", "rad", "azi", None),
        P("rad", "azi", None),
        P("rad", "azi", None),
        P("rad", "azi", None),
        P(),
    )
    return jax.shard_map(
        local,
        mesh=mesh,
        in_specs=placed,
        out_specs=(P("tm", "rad", "azi", None), P("rad", "azi", None), P()),
        check_vma=False,
    )
```

```python
import functools
import math

import jax
import jax.numpy as jnp
from jax import lax
from jax.experimental import pallas as pl
from jax.experimental.pallas import tpu as pltpu
from jax.sharding import PartitionSpec as P

STEPS = 2
SWEEPS = 8
DT_FINE = 0.25
LOWER_EDGE = 0.05
UPPER_EDGE = 1.95

BLOCKS = 8
RADS = 4
RB = 16
AB = 16
NZ = 128
ZB = NZ // BLOCKS
HALO = 2 * SWEEPS
WIN = ZB + 2 * HALO
SLICES = 32
GROUP = 2 * WIN
FIELDS = 4
ROWS = FIELDS * GROUP + 2 * ZB
PAD = 8
VMEM = 48 * 1024 * 1024
WHOLE_VMEM = 56 * 1024 * 1024


STRIDES = ((4, 64), (2, 32), (1, 8))
INNER = 8


def rows_of(half):
    for t in range(16):
        yield ((t >> 1) & 1) * 8 + half * 4 + ((t >> 3) & 1) * 2 + ((t >> 2) & 1), t & 1


def lane_groups(tiles):
    tiles = list(tiles)
    lane = lax.broadcasted_iota(jnp.int32, tiles[0].shape, 1)
    for bit, stride in STRIDES:
        low = (lane & stride) == 0
        for i in range(8):
            if i & bit:
                continue
            first, second = tiles[i], tiles[i + bit]
            if 2 * stride == NZ:
                moved = pltpu.roll(jnp.where(low, second, first), stride, 1)
                tiles[i], tiles[i + bit] = jnp.where(low, first, moved), jnp.where(low, moved, second)
            else:
                tiles[i] = jnp.where(low, first, pltpu.roll(second, stride, 1))
                tiles[i + bit] = jnp.where(low, pltpu.roll(first, NZ - stride, 1), second)
    return tiles


def block_of(group):
    return group


def pack_kernel(start_at, target_at, cond_at, material_at, current_at, out_at, start, target, cond, material, current, out, sems, sent):
    pairs = ((start_at, start), (material_at, material), (cond_at, cond), (current_at, current), (target_at, target))
    copies = [pltpu.make_async_copy(src, dst, sems.at[k]) for k, (src, dst) in enumerate(pairs)]
    for copy in copies:
        copy.start()

    def turned(read, half):
        return jnp.transpose(jnp.concatenate([read(r, pl.ds(q, 8, stride=2)) for r, q in rows_of(half)], axis=0))

    def put(field, half, read):
        edge = jnp.zeros((HALO, NZ), jnp.float32)
        padded = jnp.concatenate([edge, turned(read, half), edge], axis=0)
        for j in range(BLOCKS):
            out[j, pl.ds(field * GROUP + half * WIN, WIN), :] = padded[ZB * j : ZB * j + WIN]

    sends = []

    def send(field, size):
        rows = pl.ds(field * GROUP, size)
        sends.append(pltpu.make_async_copy(out.at[:, rows, :], out_at.at[:, rows, :], sent.at[field]))
        sends[-1].start()

    copies[0].wait()
    for half in range(2):
        put(0, half, lambda r, q: start[r, q, :])
    send(0, GROUP)
    copies[1].wait()
    for half in range(2):
        put(1, half, lambda r, q: jnp.where(material[r, q, :] == 1, 1.0, 0.0))
    send(1, GROUP)
    copies[2].wait()
    for half in range(2):
        put(2, half, lambda r, q: cond[r, q, :])
    send(2, GROUP)
    copies[3].wait()
    for half in range(2):
        put(3, half, lambda r, q: jnp.where(material[r, q, :] == 2, current[r, q, :], 0.0))
    send(3, GROUP)
    copies[4].wait()
    for half in range(2):
        flat = turned(lambda r, q: target[r, q, :], half)
        for j in range(BLOCKS):
            out[j, pl.ds(FIELDS * GROUP + half * ZB, ZB), :] = flat[ZB * j : ZB * (j + 1)]
    send(4, 2 * ZB)
    for copy in sends:
        copy.wait()


def fine_kernel(coef, got, out, static, xa, xb, rho, iron, cond, source, sat, step_d, base, a_rp, a_rm, a_ap, a_am, a_zp, a_zm):
    b0, b1, b2 = coef[0], coef[1], coef[2]
    me = lax.axis_index("rad") * 2 + lax.axis_index("azi")
    slot = lax.axis_index("tm")

    def edged(q, s):
        return q * (INNER + 2) + s + 1

    def to_x(q, s, row, value):
        xa[edged(q, s), pl.ds(PAD + row, 8), :] = value

    def to(ref):
        def put(q, s, row, value):
            ref[q * INNER + s, pl.ds(row, 8), :] = value

        return put

    def some(tile, carry):
        row = pl.multiple_of(tile * 8, 8)
        for field, dest in ((0, to_x), (1, to(iron)), (2, to(cond)), (3, to(source))):
            for half in range(2):
                rows = field * GROUP + half * WIN + row
                tiles = [got[pl.ds(pl.multiple_of(block_of(g) * ROWS + rows, 8), 8), :] for g in range(8)]
                for g, value in enumerate(lane_groups(tiles)):
                    dest(g & 1, half * 4 + (g >> 1), row, value)
        return carry

    lax.fori_loop(0, WIN // 8, some, 0)

    blank = jnp.zeros((PAD, NZ), jnp.float32)
    for i in range(2 * (INNER + 2)):
        for x in (xa, xb):
            x[i, pl.ds(0, PAD), :] = blank
            x[i, pl.ds(PAD + WIN, PAD), :] = blank
        rho[i, pl.ds(0, PAD), :] = blank + 1.0
        rho[i, pl.ds(PAD + WIN, PAD), :] = blank + 1.0

    def wrap(get, put, size, outside):
        lane = lax.broadcasted_iota(jnp.int32, (size, NZ), 1)
        for q in range(2):
            last = pltpu.roll(get(edged(q, INNER - 1)), 16, 1)
            put(edged(q, -1), jnp.where(lane < 16, outside, last))
            first = pltpu.roll(get(edged(q, 0)), NZ - 16, 1)
            put(edged(q, INNER), jnp.where(lane >= NZ - 16, outside, first))

    def wrap_x(x, z0, nz):
        rows = pl.ds(PAD + z0, nz)

        def put(i, value):
            x[i, rows, :] = value

        wrap(lambda i: x[i, rows, :], put, nz, 0.0)

    def wrap_rho(z0, nz):
        rows = pl.ds(PAD + z0, nz)

        def put(i, value):
            rho[i, rows, :] = value

        wrap(lambda i: rho[i, rows, :], put, nz, 1.0)

    def prepare(x, step, z0, nz):
        lane = lax.broadcasted_iota(jnp.int32, (nz, NZ), 1) & 15
        row = lax.broadcasted_iota(jnp.int32, (nz, NZ), 0) + (z0 - HALO) + me * ZB
        rows = pl.ds(PAD + z0, nz)
        own = pl.ds(z0, nz)

        def azimuths(ref, q, s, outside):
            beside = ref[edged(1 - q, s), rows, :]
            if q == 0:
                return beside, jnp.where(lane == 0, outside, pltpu.roll(beside, 1, 1))
            return jnp.where(lane == 15, outside, pltpu.roll(beside, NZ - 1, 1)), beside

        for q in range(2):
            for s in range(INNER):
                i, at = q * INNER + s, edged(q, s)
                radial = 0.5 * (x[at + 1, rows, :] - x[at - 1, rows, :])
                up, down = azimuths(x, q, s, 0.0)
                azimuthal = 0.5 * (up - down)
                square = radial * radial + azimuthal * azimuthal
                saturation = square / (1.0 + square)
                value = b2 + b0 * jnp.exp(b1 * saturation)
                rho[at, rows, :] = jnp.where(iron[i, own, :] > 0.5, value, 1.0)
                if step == 0:
                    sat[i] = saturation[HALO - z0 : HALO - z0 + ZB]

        wrap_rho(z0, nz)
        angle = (4.0 * math.pi / (SLICES * STEPS)) * (slot * STEPS + (step + 1)).astype(jnp.float32)
        wave = jnp.cos(jnp.full((8, NZ), angle, jnp.float32))[0:1]

        for q in range(2):
            for s in range(INNER):
                i, at = q * INNER + s, edged(q, s)
                centre = rho[at, rows, :]
                up, down = azimuths(rho, q, s, 1.0)
                rp = 0.5 * (centre + rho[at + 1, rows, :])
                rm = 0.5 * (centre + rho[at - 1, rows, :])
                ap = 0.5 * (centre + up)
                am = 0.5 * (centre + down)
                zp = 0.5 * (centre + rho[at, pl.ds(PAD + z0 + 1, nz), :])
                zm = 0.5 * (centre + rho[at, pl.ds(PAD + z0 - 1, nz), :])
                mass = cond[i, own, :] * (1.0 / DT_FINE)
                inverse = 1.0 / (mass + rp + rm + ap + am + zp + zm)
                a_rp[i, own, :] = inverse * rp
                a_rm[i, own, :] = inverse * rm
                a_ap[i, own, :] = jnp.where(lane == 15, 0.0, inverse * ap) if q else inverse * ap
                a_am[i, own, :] = inverse * am if q else jnp.where(lane == 0, 0.0, inverse * am)
                a_zp[i, own, :] = jnp.where(row == NZ - 1, 0.0, inverse * zp)
                a_zm[i, own, :] = jnp.where(row == 0, 0.0, inverse * zm)
                base[i, own, :] = inverse * (mass * x[at, rows, :] + wave * source[i, own, :])

    def sweep(x, fresh, alpha, beta, z0, nz, final):
        rows = pl.ds(PAD + z0, nz)
        own = pl.ds(z0, nz)
        lane = lax.broadcasted_iota(jnp.int32, (nz, NZ), 1)
        below = [x[edged(q, -1), rows, :] for q in range(2)]
        middle = [x[edged(q, 0), rows, :] for q in range(2)]
        for s in range(INNER):
            above = [x[edged(q, s + 1), rows, :] for q in range(2)]
            for q in range(2):
                i, at = q * INNER + s, edged(q, s)
                centre, beside = middle[q], middle[1 - q]
                rolled = pltpu.roll(beside, NZ - 1 if q else 1, 1)
                up, down = (rolled, beside) if q else (beside, rolled)
                total = base[i, own, :] - centre
                total = total + a_rp[i, own, :] * above[q]
                total = total + a_rm[i, own, :] * below[q]
                total = total + a_zp[i, own, :] * x[at, pl.ds(PAD + z0 + 1, nz), :]
                total = total + a_zm[i, own, :] * x[at, pl.ds(PAD + z0 - 1, nz), :]
                total = total + (a_ap[i, own, :] * up + a_am[i, own, :] * down)
                change = beta * total
                if alpha is not None:
                    change = change + alpha * step_d[i, own, :]
                if not final:
                    step_d[i, own, :] = change
                value = centre + change
                fresh[at, rows, :] = value
                if s == 0:
                    first = pltpu.roll(value, NZ - 16, 1)
                    fresh[edged(q, INNER), rows, :] = jnp.where(lane >= NZ - 16, 0.0, first)
                if s == INNER - 1:
                    last = pltpu.roll(value, 16, 1)
                    fresh[edged(q, -1), rows, :] = jnp.where(lane < 16, 0.0, last)
            below, middle = middle, above

    theta = 0.5 * (UPPER_EDGE + LOWER_EDGE)
    delta = 0.5 * (UPPER_EDGE - LOWER_EDGE)
    scaled = theta / delta
    ratio, alphas, betas = 1.0 / scaled, [0.0], [1.0 / theta]
    for index in range(SWEEPS - 1):
        following = 1.0 / (2.0 * scaled - ratio)
        alphas.append(following * ratio)
        betas.append(2.0 * following / delta)
        ratio = following

    def pick(values, first, at):
        chosen = jnp.float32(values[first])
        for k in range(1, (SWEEPS - first) // 2):
            chosen = jnp.where(at == k, jnp.float32(values[first + 2 * k]), chosen)
        return chosen

    wrap_x(xa, 0, WIN)
    for step in range(STEPS):
        z0 = step * SWEEPS
        nz = WIN - 2 * z0
        prepare(xa, step, z0, nz)
        sweep(xa, xb, None, betas[0], z0, nz, False)

        def pair(at, carry):
            sweep(xb, xa, pick(alphas, 1, at), pick(betas, 1, at), z0, nz, False)
            sweep(xa, xb, pick(alphas, 2, at), pick(betas, 2, at), z0, nz, False)
            return carry

        lax.fori_loop(0, (SWEEPS - 2) // 2, pair, 0)
        sweep(xb, xa, alphas[-1], betas[-1], z0 + SWEEPS, nz - 2 * SWEEPS, True)

    def put(kind, half, tile, block, value):
        out[pl.ds(((half * ZB + tile * 8) * 4 + kind) * 8 + block, 8, stride=32), :] = value

    for half in range(2):
        for tile in range(ZB // 8):
            ends = [xa[edged(g & 1, half * 4 + (g >> 1)), pl.ds(PAD + HALO + tile * 8, 8), :] for g in range(8)]
            for g, value in enumerate(lane_groups(ends)):
                put(0, half, tile, block_of(g), value)
            sats = [sat[(g & 1) * INNER + half * 4 + (g >> 1), pl.ds(tile * 8, 8), :] for g in range(8)]
            for g, value in enumerate(lane_groups(sats)):
                put(1, half, tile, block_of(g), value)
            for block in range(BLOCKS):
                rows = block * ROWS + half * WIN + HALO + tile * 8
                put(2, half, tile, block, got[pl.ds(rows, 8), :])
                rows = block * ROWS + FIELDS * GROUP + half * ZB + tile * 8
                put(3, half, tile, block, got[pl.ds(rows, 8), :])

    place = (slot // ZB) * WIN + HALO + slot % ZB
    static[pl.ds(0, 8), :] = got[pl.ds(2 * GROUP + place, 8, stride=ROWS), :]
    static[pl.ds(8, 8), :] = got[pl.ds(1 * GROUP + place, 8, stride=ROWS), :]


def chain_kernel(coef, got, static, out, jumps, resids, factors, quads):
    b0, b1, b2 = coef[0], coef[1], coef[2]
    cond = static[pl.ds(0, 8), :]
    iron = static[pl.ds(8, 8), :]
    is_iron = iron > 0.5
    dt = STEPS * DT_FINE

    def part(n, kind):
        return got[pl.ds(n * 32 + kind * 8, 8), :]

    jump = jnp.zeros((8, NZ), jnp.float32)
    for n in range(SLICES):
        growth = jnp.exp(b1 * part(n, 1))
        lumped = 6.0 * jnp.where(is_iron, b2 + b0 * growth, 1.0)
        inverse = 1.0 / (cond + dt * lumped)
        factor = cond * inverse
        end = part(n, 0) + factor * jump
        out[pl.ds(n * 24, 8, stride=3), :] = end
        jumps[n] = jump
        resids[n] = end - part(n, 3)
        factors[n] = factor
        quads[n] = inverse * inverse
        if n < SLICES - 1:
            jump = end - part(n + 1, 2)

    tail = jnp.zeros((8, NZ), jnp.float32)
    grad = jnp.zeros((8, NZ), jnp.float32)
    sums = [jnp.zeros((8, NZ), jnp.float32) for _ in range(3)]
    for n in reversed(range(SLICES)):
        saturation = part(n, 1)
        growth = jnp.exp(b1 * saturation)
        lumped = 6.0 * jnp.where(is_iron, b2 + b0 * growth, 1.0)
        slope = resids[n] + tail
        scaled = slope * jumps[n] * quads[n]
        grad = grad + scaled * (dt * lumped)
        hterm = (6.0 * scaled) * (-dt * cond) * iron
        grown = hterm * growth
        sums[0] = sums[0] + grown
        sums[1] = sums[1] + grown * (b0 * saturation)
        sums[2] = sums[2] + hterm
        tail = factors[n] * slope
    lane = lax.broadcasted_iota(jnp.int32, (8, NZ), 1)
    totals = [jnp.sum(value, keepdims=True) for value in sums]
    row = jnp.where(lane == 0, totals[0], jnp.where(lane == 1, totals[1], jnp.where(lane == 2, totals[2], 0.0)))
    for n in range(SLICES):
        out[pl.ds(n * 24 + 1, 8, stride=3), :] = grad
        out[pl.ds(n * 24 + 2, 8, stride=3), :] = row


def unpack_kernel(got, end, grad, coef_grad):
    for kind, dest in enumerate((end, grad)):
        for half in range(2):
            flat = jnp.concatenate(
                [got[pl.ds(half * ZB * 24 + j * 3 + kind, ZB, stride=24), :] for j in range(BLOCKS)], axis=0
            )
            turned = jnp.transpose(flat)
            for t, (r, q) in enumerate(rows_of(half)):
                dest[r, pl.ds(q, 8, stride=2), :] = turned[8 * t : 8 * t + 8]
    sums = jnp.sum(got[pl.ds(2, SLICES * BLOCKS, stride=3), :], axis=0, keepdims=True)
    lane = lax.broadcasted_iota(jnp.int32, (1, NZ), 1)
    count = SLICES * BLOCKS * RB * AB * NZ
    for c in range(3):
        coef_grad[c] = jnp.sum(jnp.where(lane == c, sums, 0.0)) * (1.0 / count)


def vmem():
    return pl.BlockSpec(memory_space=pltpu.VMEM)


def smem():
    return pl.BlockSpec(memory_space=pltpu.SMEM)


def call(kernel, outs, ins, scratch, out_specs=None):
    spaces = {"s": pltpu.SMEM, "v": pltpu.VMEM, "h": pltpu.HBM}
    specs = [pl.BlockSpec(memory_space=spaces[place]) for place in ins]
    return pl.pallas_call(
        kernel,
        out_shape=outs,
        in_specs=specs,
        out_specs=out_specs if out_specs is not None else jax.tree.map(lambda leaf: vmem(), outs),
        scratch_shapes=scratch,
        compiler_params=pltpu.CompilerParams(vmem_limit_bytes=WHOLE_VMEM if "h" in ins else VMEM),
    )


def shape(*dims):
    return jax.ShapeDtypeStruct(dims, jnp.float32)


def solve(bh_coef, whole):
    block = pltpu.VMEM((RB, WIN, NZ), jnp.float32)
    return call(
        fine_kernel,
        (shape(SLICES * 32, NZ), shape(16, NZ)),
        "sv",
        [
            pltpu.VMEM((2 * (INNER + 2), WIN + 2 * PAD, NZ), jnp.float32),
            pltpu.VMEM((2 * (INNER + 2), WIN + 2 * PAD, NZ), jnp.float32),
            pltpu.VMEM((2 * (INNER + 2), WIN + 2 * PAD, NZ), jnp.float32),
            block,
            block,
            block,
            pltpu.VMEM((RB, ZB, NZ), jnp.float32),
        ]
        + [block] * 8,
    )(bh_coef, whole)


def local(start_states, target, conductivity, material, current, bh_coef):
    field = pltpu.VMEM((RB, AB, NZ), jnp.float32)
    packed = call(
        pack_kernel,
        shape(BLOCKS, ROWS, NZ),
        "hhhhh",
        [field, field, field, pltpu.VMEM((RB, AB, NZ), jnp.int32), field, pltpu.VMEM((BLOCKS, ROWS, NZ), jnp.float32)]
        + [pltpu.SemaphoreType.DMA((5,))] * 2,
        out_specs=pl.BlockSpec(memory_space=pltpu.HBM),
    )(start_states[0], target[0], conductivity, material, current).reshape(BLOCKS * ROWS, NZ)
    whole = lax.all_to_all(packed, ("rad", "azi"), 0, 0, tiled=True)
    fine, static = solve(bh_coef, whole)
    slices = lax.all_to_all(fine, "tm", 0, 0, tiled=True)
    line = pltpu.VMEM((SLICES, 8, NZ), jnp.float32)
    chained = call(chain_kernel, shape(SLICES * 24, NZ), "svv", [line] * 4)(bh_coef, slices, static)
    results = lax.all_to_all(
        chained.reshape(SLICES * BLOCKS, 1, 3 * NZ), ("tm", "rad", "azi"), 0, 0, tiled=True
    ).reshape(SLICES * 24, NZ)
    end, grad, coef_grad = call(
        unpack_kernel,
        (shape(RB, AB, NZ), shape(RB, AB, NZ), shape(3)),
        "v",
        [],
        out_specs=(vmem(), vmem(), smem()),
    )(results)
    return (end[None], grad, coef_grad)


def solution(mesh):
    placed = (
        P("tm", "rad", "azi", None),
        P("tm", "rad", "azi", None),
        P("rad", "azi", None),
        P("rad", "azi", None),
        P("rad", "azi", None),
        P(),
    )
    return jax.shard_map(
        local,
        mesh=mesh,
        in_specs=placed,
        out_specs=(P("tm", "rad", "azi", None), P("rad", "azi", None), P()),
        check_vma=False,
    )
```
